256 devices in a mesh: seq: 32 (over x, z), head: 8 (over y, core).
Axes of the slice: x: 4, y: 4, z: 8, core: 2. Of those that a mesh axis runs over, the one named last changes fastest.
Arguments:
- hidden: bfloat16 [32768, 8192], P('seq'), may hold values from -27 to 27, as said below
- key_value_weight: bfloat16 [8192, 2048], P('seq', 'head'), may hold values from -0.0625 to 0.0625
- down_projection: bfloat16 [2048, 512], P('head'), may hold values from -0.125 to 0.125
- up_projection: bfloat16 [512, 2048], P(None, 'head'), may hold values from -0.25 to 0.25
- positions: int32 [32768], P('seq'), may hold values from 0 to 131071
Outputs:
- grad_down: float32 [512, 2048], P('seq', 'head')
- grad_up: float32 [512, 2048], P('seq', 'head')
- rel_error: float32 [], replicated
The draws below stay inside these ranges and needn't reach their ends.
Inputs may be any that keep to these rules, and one draw needn't show every extreme that they name: `hidden`: real-valued inputs, rows of differing scale.
All inputs are finite; a program needn't handle non-finite values.
Results may differ from the reference program's by a relative error of at most 0.0045.
Values may be sent and summed in bfloat16 or wider, within the bound.
No kernel may reach another device: no remote copies, remote signals or barrier semaphores. Data moves between devices by JAX's collectives and lax.ppermute only.
A program may use at most 64 MiB of HBM per device.

```python
import math
import jax
import jax.numpy as jnp
from jax import lax

MODEL_WIDTH = 8192
KEY_VALUE_HEADS = 8
HEAD_SIZE = 128
LATENT_RANK = 512
WINDOW_TOKENS = 32768


def draw_hidden(key, part):
    first_key, second_key = jax.random.split(key, 2)
    row_index = jnp.arange(WINDOW_TOKENS, dtype=jnp.float32)
    row_scale = jnp.exp(jax.random.uniform(second_key, (WINDOW_TOKENS, 1), jnp.float32, jnp.log(0.3), jnp.log(3.0)))
    base = jnp.clip(jax.random.normal(first_key, (WINDOW_TOKENS, MODEL_WIDTH), jnp.float32), -6.0, 6.0)
    ramp = 1.0 + 0.75 * row_index / WINDOW_TOKENS
    return (base * row_scale * ramp[:, None]).astype(jnp.bfloat16)


def plant(array, stream_key, smallest, top_value):
    spot = [jax.random.randint(jax.random.fold_in(stream_key, axis), (), 0, length) for axis, length in enumerate(array.shape)]
    widest = array.shape.index(max(array.shape))
    neighbour = spot[:widest] + [(spot[widest] + 1) % array.shape[widest]] + spot[widest + 1:]
    return array.at[tuple(spot)].set(smallest).at[tuple(neighbour)].set(top_value)


def block_scale(key, extent, cuts, low, largest):
    def one(dim, blocks):
        steps = jax.random.uniform(jax.random.fold_in(jax.random.fold_in(key, 6), dim), (blocks,), jnp.float32, low / len(cuts), largest / len(cuts))
        return jnp.repeat(jnp.exp(steps), extent[dim] // blocks).reshape((-1,) + (1,) * (len(extent) - dim - 1))

    factor_of = one(*cuts[0])
    for cut in cuts[1:]:
        factor_of = factor_of * one(*cut)
    return factor_of


def gaussian(own_key, dims, deviation, limit, cuts=(), kind=jnp.bfloat16):
    array = jax.random.normal(own_key, dims, jnp.float32) * deviation
    if len(cuts) > 0:
        array = block_scale(own_key, dims, cuts, -0.22, 0.18) * array
    return jnp.clip(array, min=-limit, max=limit).astype(kind)


def setup_inputs(seed: int = 0) -> dict:
    arg_keys = jax.random.split(jax.random.key(seed), 6)
    hidden = draw_hidden(jax.random.fold_in(arg_keys[5], 71), 0)
    key_value_weight = gaussian(arg_keys[1], (MODEL_WIDTH, 2 * KEY_VALUE_HEADS * HEAD_SIZE), MODEL_WIDTH ** -0.5, 0.0625, ((0, 32), (1, 8)))
    down_projection = gaussian(arg_keys[2], (2 * KEY_VALUE_HEADS * HEAD_SIZE, LATENT_RANK), (2 * KEY_VALUE_HEADS * HEAD_SIZE) ** -0.5, 0.125, ((0, 8),))
    up_projection = gaussian(arg_keys[3], (LATENT_RANK, 2 * KEY_VALUE_HEADS * HEAD_SIZE), LATENT_RANK ** -0.5, 0.25, ((1, 8),))
    positions = plant(jax.random.randint(arg_keys[4], (WINDOW_TOKENS,), 0, 131072), jax.random.fold_in(arg_keys[4], 1), 0, 131071).astype(jnp.int32)
    return {"hidden": hidden, "key_value_weight": key_value_weight, "down_projection": down_projection, "up_projection": up_projection, "positions": positions}


THETA = 500000.0

def rotate_targets(dense, positions):
    half_dim = HEAD_SIZE // 2
    freqs = jnp.power(jnp.float32(THETA), -(jnp.arange(half_dim, dtype=jnp.float32) * 2.0 / HEAD_SIZE))
    angle = positions.astype(jnp.float32)[:, None] * freqs[None, :]
    cosine = jnp.cos(angle)[:, None, :]
    sine = jnp.sin(angle)[:, None, :]
    shaped = dense.reshape(dense.shape[0], -1, 2, HEAD_SIZE)
    key_part = shaped[:, :, 0, :]
    first = key_part[..., :half_dim]
    second = key_part[..., half_dim:]
    turned = jnp.concatenate([first * cosine - second * sine, second * cosine + first * sine], axis=-1)
    joined = jnp.stack([turned, shaped[:, :, 1, :]], axis=2)
    return joined.reshape(dense.shape[0], -1).astype(jnp.bfloat16)

def reference(hidden, key_value_weight, down_projection, up_projection, positions):
    dense = jnp.dot(hidden, key_value_weight, preferred_element_type=jnp.float32)
    targets = rotate_targets(dense, positions)
    target_wide = targets.astype(jnp.float32)
    energy = jnp.sum(target_wide * target_wide)
    latent = jnp.dot(targets, down_projection, preferred_element_type=jnp.float32).astype(jnp.bfloat16)
    rebuilt = jnp.dot(latent, up_projection, preferred_element_type=jnp.float32)
    residual = target_wide - rebuilt
    rel_error = jnp.sum(residual * residual) / energy
    entry_items = WINDOW_TOKENS * 2 * KEY_VALUE_HEADS * HEAD_SIZE
    factor = -(entry_items / energy) / math.sqrt(WINDOW_TOKENS)
    latent_wide = latent.astype(jnp.float32)
    up_wide = up_projection.astype(jnp.float32)
    grad_up = factor * jnp.dot(latent_wide.T, residual, precision=lax.Precision.HIGHEST, preferred_element_type=jnp.float32)
    d_latent = jnp.dot(residual, up_wide.T, precision=lax.Precision.HIGHEST, preferred_element_type=jnp.float32).astype(jnp.bfloat16)
    grad_down = factor * jnp.dot(d_latent.T, targets, preferred_element_type=jnp.float32)
    return (grad_down, grad_up, rel_error)
```

```python
import math

import jax
import jax.numpy as jnp
from jax import lax
from jax.experimental import pallas as pl
from jax.experimental.pallas import tpu as pltpu
from jax.sharding import PartitionSpec as P

KEY_VALUE_HEADS = 8
HEAD_SIZE = 128
HEAD_COLUMNS = 2 * HEAD_SIZE
LATENT_RANK = 512
THETA = 500000.0
X, Z, HEADS = 4, 8, 8
SEQ = X * Z
MIB = 1024 * 1024
F32 = jnp.float32
BF16 = jnp.bfloat16


def z_shift(k):
    return [(x * Z + z, x * Z + (z + k) % Z) for x in range(X) for z in range(Z)]


def x_shift(k):
    return [(x * Z + z, ((x + k) % X) * Z + z) for x in range(X) for z in range(Z)]


def ring_z(own):
    up = down = own
    found = [(0, own)]
    for k in range(1, Z // 2):
        up, down = lax.ppermute(up, "seq", z_shift(1)), lax.ppermute(down, "seq", z_shift(-1))
        found += [(-k, up), (k, down)]
    half = own.shape[0] // 2
    first = lax.ppermute(up[:half], "seq", z_shift(1))
    second = lax.ppermute(down[half:], "seq", z_shift(-1))
    return found, (first, second)


def ring_x(own):
    up, down = lax.ppermute(own, "seq", x_shift(1)), lax.ppermute(own, "seq", x_shift(-1))
    half = own.shape[0] // 2
    first = lax.ppermute(up[:half], "seq", x_shift(1))
    second = lax.ppermute(down[half:], "seq", x_shift(-1))
    return [(0, own), (-1, up), (1, down)], (first, second)


def gather_weight(weight):
    part_rows = weight.shape[0] // 2
    part_a, part_b = weight[:part_rows], weight[part_rows:]
    a_found, a_far = ring_z(part_a)
    b_found, b_far = ring_x(part_b)
    a_order = [d for d, _ in a_found] + [Z // 2]
    b_order = [d for d, _ in b_found] + [X // 2]
    a_all = jnp.concatenate([rows for _, rows in a_found] + list(a_far), axis=0)
    b_all = jnp.concatenate([rows for _, rows in b_found] + list(b_far), axis=0)
    pieces = []
    found, (first, second) = ring_x(a_all)
    for dx, rows in found:
        pieces.append((rows, [(i * part_rows, dx, dz, 0) for i, dz in enumerate(a_order)]))
    half = len(a_order) // 2
    for rows, order in ((first, a_order[:half]), (second, a_order[half:])):
        pieces.append((rows, [(i * part_rows, X // 2, dz, 0) for i, dz in enumerate(order)]))
    found, (first, second) = ring_z(b_all)
    for dz, rows in found:
        pieces.append((rows, [(i * part_rows, dx, dz, 1) for i, dx in enumerate(b_order)]))
    half = len(b_order) // 2
    for rows, order in ((first, b_order[:half]), (second, b_order[half:])):
        pieces.append((rows, [(i * part_rows, dx, Z // 2, 1) for i, dx in enumerate(order)]))
    return pieces


def dense_targets(place, hidden, pieces, cosine, sine):
    rows, width = hidden.shape
    tile = 256
    count = len(pieces)

    def kernel(place_ref, hidden_ref, cos_ref, sin_ref, *rest):
        piece_refs, out_ref, weight_ref = rest[:count], rest[count], rest[count + 1]

        @pl.when(pl.program_id(0) == 0)
        def _():
            here = place_ref[0]
            x, z = here // Z, here % Z
            for ref, (_, entries) in zip(piece_refs, pieces):
                for row, dx, dz, part in entries:
                    owner = ((x + dx + X) % X) * Z + (z + dz + Z) % Z
                    start = pl.multiple_of(owner * 256 + part * 128, 128)
                    weight_ref[pl.ds(start, 128), :] = ref[row : row + 128, :]

        dense = jnp.dot(hidden_ref[...], weight_ref[...], preferred_element_type=F32)
        keys = dense[:, :HEAD_SIZE]
        turned = keys * cos_ref[...] + pltpu.roll(keys, HEAD_SIZE // 2, 1) * sin_ref[...]
        out_ref[:, :HEAD_SIZE] = turned.astype(BF16)
        out_ref[:, HEAD_SIZE:] = dense[:, HEAD_SIZE:].astype(BF16)

    whole = pl.BlockSpec(memory_space=pltpu.VMEM)
    return pl.pallas_call(
        kernel,
        grid=(rows // tile,),
        out_shape=jax.ShapeDtypeStruct((rows, HEAD_COLUMNS), BF16),
        in_specs=[
            pl.BlockSpec(memory_space=pltpu.SMEM),
            pl.BlockSpec((tile, width), lambda i: (i, 0)),
            pl.BlockSpec((tile, HEAD_SIZE), lambda i: (i, 0)),
            pl.BlockSpec((tile, HEAD_SIZE), lambda i: (i, 0)),
        ]
        + [whole] * count,
        out_specs=pl.BlockSpec((tile, HEAD_COLUMNS), lambda i: (i, 0)),
        scratch_shapes=[pltpu.VMEM((width, HEAD_COLUMNS), BF16)],
        compiler_params=pltpu.CompilerParams(vmem_limit_bytes=40 * MIB),
    )(place, hidden, cosine, sine, *[rows_ for rows_, _ in pieces])


def split3(value):
    high = value.astype(BF16).astype(F32)
    middle = (value - high).astype(BF16).astype(F32)
    return high, middle, value - high - middle


def spread(lane, first, second):
    out = jnp.zeros(lane.shape, F32)
    for i, part in enumerate((*split3(first), *split3(second))):
        out = jnp.where(lane == i, part, out)
    return out


def token_share(targets, down, up):
    heads, tokens, columns = targets.shape
    rank = down.shape[1]

    def kernel(t_ref, d_ref, u_ref, out_ref):
        total = jnp.zeros((tokens, rank), F32)
        for h in range(heads):
            total += jnp.dot(t_ref[h], d_ref[h * columns : (h + 1) * columns, :], preferred_element_type=F32)
        latent = total.astype(BF16)
        grad = jnp.zeros((tokens, rank), F32)
        energy = jnp.zeros((tokens, columns), F32)
        misfit = jnp.zeros((tokens, columns), F32)
        nt = (((1,), (1,)), ((), ()))
        for h in range(heads):
            wide = t_ref[h].astype(F32)
            rest = wide - jnp.dot(latent, u_ref[h], preferred_element_type=F32)
            energy += wide * wide
            misfit += rest * rest
            high = rest.astype(BF16)
            low = (rest - high.astype(F32)).astype(BF16)
            grad += lax.dot_general(high, u_ref[h], nt, preferred_element_type=F32)
            grad += lax.dot_general(low, u_ref[h], nt, preferred_element_type=F32)
        out_ref[0:tokens, 0:rank] = latent
        out_ref[0:tokens, rank : 2 * rank] = grad.astype(BF16)
        lane = lax.broadcasted_iota(jnp.int32, (16, 2 * rank), 1)
        sums = spread(lane, jnp.sum(energy), jnp.sum(misfit))
        out_ref[tokens : tokens + 16, :] = sums.astype(BF16)

    whole = pl.BlockSpec(memory_space=pltpu.VMEM)
    return pl.pallas_call(
        kernel,
        out_shape=jax.ShapeDtypeStruct((tokens + 16, 2 * rank), BF16),
        in_specs=[whole] * 3,
        out_specs=whole,
        compiler_params=pltpu.CompilerParams(vmem_limit_bytes=24 * MIB),
    )(targets, down, up)


def factor_grads(latents, targets, up):
    shares, padded, width = latents.shape
    tokens = padded - 16
    rank, columns = up.shape
    rows = rank // SEQ
    tn = (((0,), (0,)), ((), ()))

    def kernel(lat_ref, t_ref, u_ref, out_ref):
        grad_down = jnp.zeros((rank, columns), F32)
        grad_up = jnp.zeros((rank, columns), F32)
        sums = jnp.zeros((1, 128), F32)
        for j in range(shares):
            latent = lat_ref[j, 0:tokens, 0:rank]
            grad = lat_ref[j, 0:tokens, rank : 2 * rank]
            block = t_ref[j * tokens : (j + 1) * tokens, :]
            rest = block.astype(F32) - jnp.dot(latent, u_ref[...], preferred_element_type=F32)
            high = rest.astype(BF16)
            low = (rest - high.astype(F32)).astype(BF16)
            grad_up += lax.dot_general(latent, high, tn, preferred_element_type=F32)
            grad_up += lax.dot_general(latent, low, tn, preferred_element_type=F32)
            grad_down += lax.dot_general(grad, block, tn, preferred_element_type=F32)
            sums += lat_ref[j, tokens : tokens + 16, 0:128].astype(F32)[0:1, :]
        lane = lax.broadcasted_iota(jnp.int32, (1, 128), 1)
        energy = jnp.sum(jnp.where(lane < 3, sums, 0.0))
        misfit = jnp.sum(jnp.where((lane >= 3) & (lane < 6), sums, 0.0))
        lane = lax.broadcasted_iota(jnp.int32, (rows, 128), 1)
        tail = spread(lane, energy, misfit).astype(BF16)
        for s in range(SEQ):
            out_ref[s, :, 0:columns] = grad_down[s * rows : (s + 1) * rows, :].astype(BF16)
            out_ref[s, :, columns : 2 * columns] = grad_up[s * rows : (s + 1) * rows, :].astype(BF16)
            out_ref[s, :, 2 * columns :] = tail

    whole = pl.BlockSpec(memory_space=pltpu.VMEM)
    return pl.pallas_call(
        kernel,
        out_shape=jax.ShapeDtypeStruct((SEQ, rows, 2 * columns + 128), BF16),
        in_specs=[whole] * 3,
        out_specs=whole,
        compiler_params=pltpu.CompilerParams(vmem_limit_bytes=24 * MIB),
    )(latents, targets, up)


def finish(parts, columns, tokens_all):
    blocks, rows, width = parts.shape
    entries = tokens_all * 2 * KEY_VALUE_HEADS * HEAD_SIZE

    def kernel(p_ref, down_ref, up_ref, rel_ref):
        total = jnp.zeros((rows, width), F32)
        for s in range(blocks):
            total += p_ref[s].astype(F32)
        tail = total[0:1, 2 * columns :]
        lane = lax.broadcasted_iota(jnp.int32, tail.shape, 1)
        energy = jnp.sum(jnp.where(lane < 3, tail, 0.0), keepdims=True)
        misfit = jnp.sum(jnp.where((lane >= 3) & (lane < 6), tail, 0.0), keepdims=True)
        factor = -(entries / energy) / math.sqrt(tokens_all)
        down_ref[...] = total[:, :columns] * factor
        up_ref[...] = total[:, columns : 2 * columns] * factor
        rel_ref[...] = misfit / energy

    whole = pl.BlockSpec(memory_space=pltpu.VMEM)
    return pl.pallas_call(
        kernel,
        out_shape=[
            jax.ShapeDtypeStruct((rows, columns), F32),
            jax.ShapeDtypeStruct((rows, columns), F32),
            jax.ShapeDtypeStruct((1, 1), F32),
        ],
        in_specs=[whole],
        out_specs=[whole] * 3,
    )(parts)


def per_device(hidden, key_value_weight, down_projection, up_projection, positions):
    rows_here = hidden.shape[0]
    tokens_all = lax.axis_size("seq") * rows_here
    down = lax.all_gather(down_projection, "head", axis=0, tiled=True)
    up = lax.all_gather(up_projection, "head", axis=0)
    half_dim = HEAD_SIZE // 2
    freqs = jnp.power(F32(THETA), -(jnp.arange(half_dim, dtype=F32) * 2.0 / HEAD_SIZE))
    angle = positions.astype(F32)[:, None] * freqs[None, :]
    cosine, sine = jnp.cos(angle), jnp.sin(angle)
    cosine = jnp.concatenate([cosine, cosine], axis=1)
    sine = jnp.concatenate([-sine, sine], axis=1)
    place = lax.axis_index("seq").astype(jnp.int32)[None]
    targets = dense_targets(place, hidden, gather_weight(key_value_weight), cosine, sine)
    shares = targets.reshape(HEADS, rows_here // HEADS, HEAD_COLUMNS)
    shares = lax.all_to_all(shares, "head", 0, 0)
    latents = lax.all_gather(token_share(shares, down, up), "head", axis=0)
    parts = factor_grads(latents, targets, up_projection)
    parts = lax.all_to_all(parts, "seq", 0, 0)
    grad_down, grad_up, rel_error = finish(parts, HEAD_COLUMNS, tokens_all)
    return grad_down, grad_up, rel_error.reshape(())


def solution(mesh):
    return jax.shard_map(
        per_device,
        mesh=mesh,
        in_specs=(P("seq", None), P("seq", "head"), P("head", None), P(None, "head"), P("seq")),
        out_specs=(P("seq", "head"), P("seq", "head"), P()),
        check_vma=False,
    )
```

```python
import math

import jax
import jax.numpy as jnp
from jax import lax
from jax.experimental import pallas as pl
from jax.experimental.pallas import tpu as pltpu
from jax.sharding import PartitionSpec as P

KEY_VALUE_HEADS = 8
HEAD_SIZE = 128
HEAD_COLUMNS = 2 * HEAD_SIZE
LATENT_RANK = 512
THETA = 500000.0
X, Y, Z, HEADS = 4, 4, 8, 8
SEQ = X * Z
MIB = 1024 * 1024
F32 = jnp.float32
BF16 = jnp.bfloat16


def z_shift(k):
    return [(x * Z + z, x * Z + (z + k) % Z) for x in range(X) for z in range(Z)]


def x_shift(k):
    return [(x * Z + z, ((x + k) % X) * Z + z) for x in range(X) for z in range(Z)]


def y_shift(k):
    return [(y * 2 + c, ((y + k) % Y) * 2 + c) for y in range(Y) for c in range(2)]


def ring_z(own):
    up = down = own
    found = [(0, own)]
    for k in range(1, Z // 2):
        up, down = lax.ppermute(up, "seq", z_shift(1)), lax.ppermute(down, "seq", z_shift(-1))
        found += [(-k, up), (k, down)]
    half = own.shape[0] // 2
    first = lax.ppermute(up[:half], "seq", z_shift(1))
    second = lax.ppermute(down[half:], "seq", z_shift(-1))
    return found, (first, second)


def ring_x(own, direct):
    up, down = lax.ppermute(own, "seq", x_shift(1)), lax.ppermute(own, "seq", x_shift(-1))
    found = [(0, own), (-1, up), (1, down)]
    if direct:
        return found, (lax.ppermute(own, "seq", x_shift(X // 2)),)
    half = own.shape[0] // 2
    first = lax.ppermute(up[:half], "seq", x_shift(1))
    second = lax.ppermute(down[half:], "seq", x_shift(-1))
    return found, (first, second)


def gather_weight(weight):
    part_rows = weight.shape[0] // 2
    part_a, part_b = weight[:part_rows], weight[part_rows:]
    b_found, b_far = ring_x(part_b, True)
    a_found, a_far = ring_z(part_a)
    a_order = [d for d, _ in a_found] + [Z // 2]
    b_order = [d for d, _ in b_found] + [X // 2]
    a_all = jnp.concatenate([rows for _, rows in a_found] + list(a_far), axis=0)
    b_all = jnp.concatenate([rows for _, rows in b_found] + list(b_far), axis=0)
    a_pieces, a_last = ring_x(a_all, False)
    b_pieces, b_last = ring_z(b_all)
    a_pieces = [(rows, [(dx, dz, 0) for dz in a_order]) for dx, rows in a_pieces]
    b_pieces = [(rows, [(dx, dz, 1) for dx in b_order]) for dz, rows in b_pieces]
    half = len(a_order) // 2
    last = [(rows, [(X // 2, dz, 0) for dz in a_order[i * half : (i + 1) * half]]) for i, rows in enumerate(a_last)]
    half = len(b_order) // 2
    last += [(rows, [(dx, Z // 2, 1) for dx in b_order[i * half : (i + 1) * half]]) for i, rows in enumerate(b_last)]
    return [b_pieces[0:1], b_pieces[1:3], a_pieces[0:1], b_pieces[3:5], a_pieces[1:3], b_pieces[5:7], last]


def dense_step(place, hidden, group, total, turn):
    rows = hidden.shape[0]
    columns = group[0][0].shape[1]
    blocks = [entry for _, entries in group for entry in entries]
    width = 128 * len(blocks)
    extra = [] if total is None else [total]
    extra += [] if turn is None else list(turn)

    def kernel(place_ref, hidden_ref, *rest):
        piece_refs, rest = rest[: len(group)], rest[len(group) :]
        extra_refs, (out_ref, block_ref, sems) = rest[: len(extra)], rest[len(extra) :]
        here = place_ref[0]
        x, z = here // Z, here % Z
        copies = []
        for i, (dx, dz, part) in enumerate(blocks):
            owner = ((x + dx + X) % X) * Z + (z + dz + Z) % Z
            start = pl.multiple_of(owner * 256 + part * 128, 128)
            copies.append(
                pltpu.make_async_copy(
                    hidden_ref.at[:, pl.ds(start, 128)], block_ref.at[:, i * 128 : (i + 1) * 128], sems.at[i]
                )
            )
        for copy in copies:
            copy.start()
        for copy in copies:
            copy.wait()
        tile = 256
        for row in range(0, rows, tile):
            here_rows = slice(row, row + tile)
            dense = jnp.zeros((tile, columns), F32) if total is None else extra_refs[0][here_rows, :]
            start = 0
            for ref in piece_refs:
                depth = ref.shape[0]
                dense += jnp.dot(block_ref[here_rows, start : start + depth], ref[...], preferred_element_type=F32)
                start += depth
            if turn is None:
                out_ref[here_rows, :] = dense
            else:
                cos_ref, sin_ref = extra_refs[-2:]
                keys = dense[:, :HEAD_SIZE]
                turned = keys * cos_ref[here_rows, :] + pltpu.roll(keys, HEAD_SIZE // 2, 1) * sin_ref[here_rows, :]
                out_ref[here_rows, :HEAD_SIZE] = turned.astype(BF16)
                out_ref[here_rows, HEAD_SIZE:] = dense[:, HEAD_SIZE:].astype(BF16)

    whole = pl.BlockSpec(memory_space=pltpu.VMEM)
    return pl.pallas_call(
        kernel,
        out_shape=jax.ShapeDtypeStruct((rows, columns), F32 if turn is None else BF16),
        in_specs=[pl.BlockSpec(memory_space=pltpu.SMEM), pl.BlockSpec(memory_space=pl.ANY)]
        + [whole] * (len(group) + len(extra)),
        out_specs=whole,
        scratch_shapes=[pltpu.VMEM((rows, width), BF16), pltpu.SemaphoreType.DMA((len(blocks),))],
        compiler_params=pltpu.CompilerParams(vmem_limit_bytes=16 * MIB),
        cost_estimate=pl.CostEstimate(
            flops=2 * rows * width * columns, bytes_accessed=2 * rows * width, transcendentals=0
        ),
    )(place, hidden, *[rows_ for rows_, _ in group], *extra)


def split3(value):
    high = value.astype(BF16).astype(F32)
    middle = (value - high).astype(BF16).astype(F32)
    return high, middle, value - high - middle


def spread(lane, first, second):
    out = jnp.zeros(lane.shape, F32)
    for i, part in enumerate((*split3(first), *split3(second))):
        out = jnp.where(lane == i, part, out)
    return out


def head_products(heads, both, pieces, total):
    tokens, columns = pieces[0].shape
    rank = both.shape[2] // 2
    first = total is None
    extra = [] if first else [total]

    def kernel(heads_ref, both_ref, *rest):
        piece_refs, rest = rest[: len(pieces)], rest[len(pieces) :]
        extra_refs, out_refs = rest[: len(extra)], rest[len(extra) :]
        out_ref = out_refs[0]
        tile = 256

        def rows_of(i, carry):
            rows = pl.ds(pl.multiple_of(i * tile, tile), tile)
            products = jnp.zeros((tile, 2 * rank), F32) if first else extra_refs[0][rows, : 2 * rank]
            squares = jnp.zeros((tile, 128), F32) if first else extra_refs[0][rows, 2 * rank :]
            for k, ref in enumerate(piece_refs):
                block = ref[rows, :]
                products += jnp.dot(block, both_ref[heads_ref[k]], preferred_element_type=F32)
                wide = block.astype(F32)
                for c in range(0, columns, 128):
                    squares += wide[:, c : c + 128] * wide[:, c : c + 128]
            out_ref[rows, : 2 * rank] = products
            out_ref[rows, 2 * rank :] = squares
            return carry

        lax.fori_loop(0, tokens // tile, rows_of, 0)
        if first:
            gram = jnp.zeros((rank, rank), F32)
            for h in range(both.shape[0]):
                part = both_ref[h, :, rank:]
                gram += lax.dot_general(part, part, (((0,), (0,)), ((), ())), preferred_element_type=F32)
            for i, term in enumerate(split3(gram)):
                out_refs[1][i] = term.astype(BF16)

    whole = pl.BlockSpec(memory_space=pltpu.VMEM)
    out_shape = [jax.ShapeDtypeStruct((tokens, 2 * rank + 128), F32)]
    if first:
        out_shape.append(jax.ShapeDtypeStruct((3, rank, rank), BF16))
    return pl.pallas_call(
        kernel,
        out_shape=out_shape,
        in_specs=[pl.BlockSpec(memory_space=pltpu.SMEM)] + [whole] * (1 + len(pieces) + len(extra)),
        out_specs=[whole] * len(out_shape),
        compiler_params=pltpu.CompilerParams(vmem_limit_bytes=32 * MIB),
        cost_estimate=pl.CostEstimate(
            flops=4 * tokens * columns * rank * len(pieces), bytes_accessed=2 * tokens * columns, transcendentals=0
        ),
    )(heads, both, *pieces, *extra)


def factor_grads(heads, both, far, total, gram, targets, up):
    tokens, columns = targets.shape
    rank = up.shape[0]
    rows_out = rank // SEQ
    half = tokens // 2
    tn = (((0,), (0,)), ((), ()))

    def kernel(heads_ref, both_ref, far0, far1, far2, far3, total_ref, gram_ref, t_ref, u_ref, out_ref, down_ref, upg_ref, sum_ref):
        tile = 256
        down_ref[...] = jnp.zeros((rank, columns), F32)
        upg_ref[...] = jnp.zeros((rank, columns), F32)
        sum_ref[...] = jnp.zeros((16, 128), F32)

        def half_of(base, far_refs):
            def rows_of(i, carry):
                inner = pl.ds(pl.multiple_of(i * tile, tile), tile)
                rows = pl.ds(pl.multiple_of(base + i * tile, tile), tile)
                products = total_ref[rows, : 2 * rank]
                squares = total_ref[rows, 2 * rank :]
                for k, ref in enumerate(far_refs):
                    block = ref[inner, :]
                    products += jnp.dot(block, both_ref[heads_ref[k]], preferred_element_type=F32)
                    wide = block.astype(F32)
                    for c in range(0, columns, 128):
                        squares += wide[:, c : c + 128] * wide[:, c : c + 128]
                latent = products[:, :rank].astype(BF16)
                across = products[:, rank:]
                grad = across
                for k in range(3):
                    grad -= jnp.dot(latent, gram_ref[k], preferred_element_type=F32)
                fit = latent.astype(F32) * (across + grad)
                energy = jnp.sum(squares, axis=1, keepdims=True)
                misfit = energy - jnp.sum(fit, axis=1, keepdims=True)
                own = t_ref[rows, :]
                rest = own.astype(F32) - jnp.dot(latent, u_ref[...], preferred_element_type=F32)
                high = rest.astype(BF16)
                low = (rest - high.astype(F32)).astype(BF16)
                upg_ref[...] += lax.dot_general(latent, high, tn, preferred_element_type=F32) + lax.dot_general(
                    latent, low, tn, preferred_element_type=F32
                )
                down_ref[...] += lax.dot_general(grad.astype(BF16), own, tn, preferred_element_type=F32)
                lane = lax.broadcasted_iota(jnp.int32, (1, 128), 1)
                sum_ref[0:1, :] += jnp.where(lane == 0, jnp.sum(energy), jnp.where(lane == 1, jnp.sum(misfit), 0.0))
                return carry

            lax.fori_loop(0, half // tile, rows_of, 0)

        half_of(0, (far0, far2))
        half_of(half, (far1, far3))
        lane = lax.broadcasted_iota(jnp.int32, (1, 128), 1)
        energy = jnp.sum(jnp.where(lane == 0, sum_ref[0:1, :], 0.0))
        misfit = jnp.sum(jnp.where(lane == 1, sum_ref[0:1, :], 0.0))
        tail = spread(lax.broadcasted_iota(jnp.int32, (rows_out, 128), 1), energy, misfit).astype(BF16)
        for s in range(SEQ):
            rows = slice(s * rows_out, (s + 1) * rows_out)
            out_ref[s, :, 0:columns] = down_ref[rows, :].astype(BF16)
            out_ref[s, :, columns : 2 * columns] = upg_ref[rows, :].astype(BF16)
            out_ref[s, :, 2 * columns :] = tail

    whole = pl.BlockSpec(memory_space=pltpu.VMEM)
    return pl.pallas_call(
        kernel,
        out_shape=jax.ShapeDtypeStruct((SEQ, rows_out, 2 * columns + 128), BF16),
        in_specs=[pl.BlockSpec(memory_space=pltpu.SMEM)] + [whole] * 9,
        out_specs=whole,
        scratch_shapes=[
            pltpu.VMEM((rank, columns), F32),
            pltpu.VMEM((rank, columns), F32),
            pltpu.VMEM((16, 128), F32),
        ],
        compiler_params=pltpu.CompilerParams(vmem_limit_bytes=32 * MIB),
    )(heads, both, *far, total, gram, targets, up)


def finish(parts, columns, tokens_all):
    blocks, rows, width = parts.shape
    entries = tokens_all * 2 * KEY_VALUE_HEADS * HEAD_SIZE

    def kernel(p_ref, down_ref, up_ref, rel_ref):
        total = jnp.zeros((rows, width), F32)
        for s in range(blocks):
            total += p_ref[s].astype(F32)
        tail = total[0:1, 2 * columns :]
        lane = lax.broadcasted_iota(jnp.int32, tail.shape, 1)
        energy = jnp.sum(jnp.where(lane < 3, tail, 0.0), keepdims=True)
        misfit = jnp.sum(jnp.where((lane >= 3) & (lane < 6), tail, 0.0), keepdims=True)
        factor = -(entries / energy) / math.sqrt(tokens_all)
        down_ref[...] = total[:, :columns] * factor
        up_ref[...] = total[:, columns : 2 * columns] * factor
        rel_ref[...] = misfit / energy

    whole = pl.BlockSpec(memory_space=pltpu.VMEM)
    return pl.pallas_call(
        kernel,
        out_shape=[
            jax.ShapeDtypeStruct((rows, columns), F32),
            jax.ShapeDtypeStruct((rows, columns), F32),
            jax.ShapeDtypeStruct((1, 1), F32),
        ],
        in_specs=[whole],
        out_specs=[whole] * 3,
    )(parts)


def per_device(hidden, key_value_weight, down_projection, up_projection, positions):
    rows_here = hidden.shape[0]
    tokens_all = lax.axis_size("seq") * rows_here
    both = jnp.concatenate([down_projection, up_projection.T], axis=1)
    both = lax.all_gather(both, "head", axis=0)
    half_dim = HEAD_SIZE // 2
    freqs = jnp.power(F32(THETA), -(jnp.arange(half_dim, dtype=F32) * 2.0 / HEAD_SIZE))
    angle = positions.astype(F32)[:, None] * freqs[None, :]
    cosine, sine = jnp.cos(angle), jnp.sin(angle)
    cosine = jnp.concatenate([cosine, cosine], axis=1)
    sine = jnp.concatenate([-sine, sine], axis=1)
    place = lax.axis_index("seq").astype(jnp.int32)[None]
    targets = None
    groups = gather_weight(key_value_weight)
    for i, group in enumerate(groups):
        last = i == len(groups) - 1
        targets = dense_step(place, hidden, group, targets, (cosine, sine) if last else None)
    head = lax.axis_index("head").astype(jnp.int32)
    y, core = head // 2, head % 2

    def pair(dy):
        other = (y + dy + Y) % Y
        return [other * 2 + core, other * 2 + 1 - core]

    half = rows_here // 2
    swap = [(h, h ^ 1) for h in range(HEADS)]
    below = lax.ppermute(targets, "head", y_shift(1))
    above = lax.ppermute(targets, "head", y_shift(-1))
    partner = lax.ppermute(targets, "head", swap)
    total, gram = head_products(jnp.stack(pair(0)), both, [targets, partner], None)
    far = [lax.ppermute(below[:half], "head", y_shift(1)), lax.ppermute(above[half:], "head", y_shift(-1))]
    pieces = [below, lax.ppermute(below, "head", swap), above, lax.ppermute(above, "head", swap)]
    (total,) = head_products(jnp.stack(pair(-1) + pair(1)), both, pieces, total)
    far += [lax.ppermute(rows, "head", swap) for rows in far]
    parts = factor_grads(jnp.stack(pair(Y // 2)), both, far, total, gram, targets, up_projection)
    parts = lax.all_to_all(parts, "seq", 0, 0)
    grad_down, grad_up, rel_error = finish(parts, HEAD_COLUMNS, tokens_all)
    return grad_down, grad_up, rel_error.reshape(())


def solution(mesh):
    return jax.shard_map(
        per_device,
        mesh=mesh,
        in_specs=(P("seq", None), P("seq", "head"), P("head", None), P(None, "head"), P("seq")),
        out_specs=(P("seq", "head"), P("seq", "head"), P()),
        check_vma=False,
    )
```

```python
import math

import jax
import jax.numpy as jnp
from jax import lax
from jax.experimental import pallas as pl
from jax.experimental.pallas import tpu as pltpu
from jax.sharding import PartitionSpec as P

KEY_VALUE_HEADS = 8
HEAD_SIZE = 128
HEAD_COLUMNS = 2 * HEAD_SIZE
LATENT_RANK = 512
THETA = 500000.0
X, Y, Z, HEADS = 4, 4, 8, 8
SEQ = X * Z
MIB = 1024 * 1024
F32 = jnp.float32
BF16 = jnp.bfloat16


def z_shift(k):
    return [(x * Z + z, x * Z + (z + k) % Z) for x in range(X) for z in range(Z)]


def x_shift(k):
    return [(x * Z + z, ((x + k) % X) * Z + z) for x in range(X) for z in range(Z)]


def y_shift(k):
    return [(y * 2 + c, ((y + k) % Y) * 2 + c) for y in range(Y) for c in range(2)]


def ring_z(own):
    up = down = own
    found = [(0, own)]
    for k in range(1, Z // 2):
        up, down = lax.ppermute(up, "seq", z_shift(1)), lax.ppermute(down, "seq", z_shift(-1))
        found += [(-k, up), (k, down)]
    half = own.shape[0] // 2
    first = lax.ppermute(up[:half], "seq", z_shift(1))
    second = lax.ppermute(down[half:], "seq", z_shift(-1))
    return found, (first, second)


def ring_x(own, direct):
    up, down = lax.ppermute(own, "seq", x_shift(1)), lax.ppermute(own, "seq", x_shift(-1))
    found = [(0, own), (-1, up), (1, down)]
    if direct:
        return found, (lax.ppermute(own, "seq", x_shift(X // 2)),)
    half = own.shape[0] // 2
    first = lax.ppermute(up[:half], "seq", x_shift(1))
    second = lax.ppermute(down[half:], "seq", x_shift(-1))
    return found, (first, second)


def gather_weight(weight):
    part_rows = weight.shape[0] // 2
    part_a, part_b = weight[:part_rows], weight[part_rows:]
    b_found, b_far = ring_x(part_b, True)
    a_found, a_far = ring_z(part_a)
    a_order = [d for d, _ in a_found] + [Z // 2]
    b_order = [d for d, _ in b_found] + [X // 2]
    a_all = jnp.concatenate([rows for _, rows in a_found] + list(a_far), axis=0)
    b_all = jnp.concatenate([rows for _, rows in b_found] + list(b_far), axis=0)
    a_pieces, a_last = ring_x(a_all, False)
    b_pieces, b_last = ring_z(b_all)
    a_pieces = [(rows, [(dx, dz, 0) for dz in a_order]) for dx, rows in a_pieces]
    b_pieces = [(rows, [(dx, dz, 1) for dx in b_order]) for dz, rows in b_pieces]
    half = len(a_order) // 2
    last = [(rows, [(X // 2, dz, 0) for dz in a_order[i * half : (i + 1) * half]]) for i, rows in enumerate(a_last)]
    half = len(b_order) // 2
    last += [(rows, [(dx, Z // 2, 1) for dx in b_order[i * half : (i + 1) * half]]) for i, rows in enumerate(b_last)]
    return [b_pieces + a_pieces, last]


def dense_step(hidden, group, total, turn):
    rows = hidden.shape[0]
    columns = group[0][0].shape[1]
    blocks = [entry for _, entries in group for entry in entries]
    width = 128 * len(blocks)
    extra = [] if total is None else [total]
    extra += [] if turn is None else list(turn)

    def kernel(hidden_ref, *rest):
        piece_refs, rest = rest[: len(group)], rest[len(group) :]
        extra_refs, (out_ref, block_ref, sum_ref, sems) = rest[: len(extra)], rest[len(extra) :]
        here = lax.axis_index("seq")
        x, z = here // Z, here % Z
        copies = []
        for i, (dx, dz, part) in enumerate(blocks):
            owner = ((x + dx + X) % X) * Z + (z + dz + Z) % Z
            start = pl.multiple_of(owner * 256 + part * 128, 128)
            copies.append(
                pltpu.make_async_copy(
                    hidden_ref.at[:, pl.ds(start, 128)], block_ref.at[:, i * 128 : (i + 1) * 128], sems.at[i]
                )
            )
        for copy in copies:
            copy.start()
        if total is None:
            sum_ref[...] = jnp.zeros((rows, columns), F32)
        else:
            sum_ref[...] = extra_refs[0][...]
        start = 0
        for ref in piece_refs:
            depth = ref.shape[0]
            for copy in copies[start // 128 : (start + depth) // 128]:
                copy.wait()
            sum_ref[...] += jnp.dot(block_ref[:, start : start + depth], ref[...], preferred_element_type=F32)
            start += depth
        tile = 256
        for row in range(0, rows, tile):
            here_rows = slice(row, row + tile)
            dense = sum_ref[here_rows, :]
            if turn is None:
                out_ref[here_rows, :] = dense
            else:
                cos_ref, sin_ref = extra_refs[-2:]
                keys = dense[:, :HEAD_SIZE]
                turned = keys * cos_ref[here_rows, :] + pltpu.roll(keys, HEAD_SIZE // 2, 1) * sin_ref[here_rows, :]
                out_ref[here_rows, :HEAD_SIZE] = turned.astype(BF16)
                out_ref[here_rows, HEAD_SIZE:] = dense[:, HEAD_SIZE:].astype(BF16)

    whole = pl.BlockSpec(memory_space=pltpu.VMEM)
    return pl.pallas_call(
        kernel,
        out_shape=jax.ShapeDtypeStruct((rows, columns), F32 if turn is None else BF16),
        in_specs=[pl.BlockSpec(memory_space=pltpu.HBM)]
        + [whole] * (len(group) + len(extra)),
        out_specs=whole,
        scratch_shapes=[
            pltpu.VMEM((rows, width), BF16),
            pltpu.VMEM((rows, columns), F32),
            pltpu.SemaphoreType.DMA((len(blocks),)),
        ],
        compiler_params=pltpu.CompilerParams(vmem_limit_bytes=48 * MIB),
        cost_estimate=pl.CostEstimate(
            flops=2 * rows * width * columns, bytes_accessed=2 * rows * width, transcendentals=0
        ),
    )(hidden, *[rows_ for rows_, _ in group], *extra)


def split3(value):
    high = value.astype(BF16).astype(F32)
    middle = (value - high).astype(BF16).astype(F32)
    return high, middle, value - high - middle


def spread(lane, first, second):
    out = jnp.zeros(lane.shape, F32)
    for i, part in enumerate((*split3(first), *split3(second))):
        out = jnp.where(lane == i, part, out)
    return out


def heads_at(offsets):
    head = lax.axis_index("head")
    y, core = head // 2, head % 2
    heads = []
    for dy in offsets:
        first = ((y + dy + Y) % Y) * 2
        heads += [first + core, first + 1 - core]
    return heads


def head_factors(down, up):
    columns, rank = down.shape

    def kernel(d_ref, u_ref, out_ref):
        out_ref[:, :rank] = d_ref[...]
        out_ref[:, rank:] = u_ref[...].astype(F32).T.astype(BF16)

    whole = pl.BlockSpec(memory_space=pltpu.VMEM)
    return pl.pallas_call(
        kernel,
        out_shape=jax.ShapeDtypeStruct((columns, 2 * rank), BF16),
        in_specs=[whole] * 2,
        out_specs=whole,
        compiler_params=pltpu.CompilerParams(vmem_limit_bytes=4 * MIB),
    )(down, up)


def head_products(offsets, both, pieces, total):
    tokens, columns = pieces[0].shape
    rank = both.shape[2] // 2
    first = total is None
    extra = [] if first else [total]

    def kernel(both_ref, *rest):
        heads = heads_at(offsets)
        piece_refs, rest = rest[: len(pieces)], rest[len(pieces) :]
        extra_refs, out_refs = rest[: len(extra)], rest[len(extra) :]
        out_ref = out_refs[0]
        tile = 256

        def rows_of(i, carry):
            rows = pl.ds(pl.multiple_of(i * tile, tile), tile)
            products = jnp.zeros((tile, 2 * rank), F32) if first else extra_refs[0][rows, : 2 * rank]
            squares = jnp.zeros((tile, 128), F32) if first else extra_refs[0][rows, 2 * rank :]
            for k, ref in enumerate(piece_refs):
                block = ref[rows, :]
                products += jnp.dot(block, both_ref[heads[k]], preferred_element_type=F32)
                wide = block.astype(F32)
                for c in range(0, columns, 128):
                    squares += wide[:, c : c + 128] * wide[:, c : c + 128]
            out_ref[rows, : 2 * rank] = products
            out_ref[rows, 2 * rank :] = squares
            return carry

        lax.fori_loop(0, tokens // tile, rows_of, 0)
        if first:
            gram = jnp.zeros((rank, rank), F32)
            for h in range(both.shape[0]):
                part = both_ref[h, :, rank:]
                gram += lax.dot_general(part, part, (((0,), (0,)), ((), ())), preferred_element_type=F32)
            for i, term in enumerate(split3(gram)):
                out_refs[1][i] = term.astype(BF16)

    whole = pl.BlockSpec(memory_space=pltpu.VMEM)
    out_shape = [jax.ShapeDtypeStruct((tokens, 2 * rank + 128), F32)]
    if first:
        out_shape.append(jax.ShapeDtypeStruct((3, rank, rank), BF16))
    return pl.pallas_call(
        kernel,
        out_shape=out_shape,
        in_specs=[whole] * (1 + len(pieces) + len(extra)),
        out_specs=[whole] * len(out_shape),
        compiler_params=pltpu.CompilerParams(vmem_limit_bytes=24 * MIB),
        cost_estimate=pl.CostEstimate(
            flops=4 * tokens * columns * rank * len(pieces), bytes_accessed=2 * tokens * columns, transcendentals=0
        ),
    )(both, *pieces, *extra)


def factor_grads(both, far, total, gram, targets, up):
    tokens, columns = targets.shape
    rank = up.shape[0]
    rows_out = rank // SEQ
    half = tokens // 2
    tn = (((0,), (0,)), ((), ()))

    def kernel(both_ref, far0, far1, far2, far3, total_ref, gram_ref, t_ref, u_ref, out_ref, down_ref, upg_ref, sum_ref):
        tile = 256
        heads = heads_at((Y // 2,))
        down_ref[...] = jnp.zeros((rank, columns), F32)
        upg_ref[...] = jnp.zeros((rank, columns), F32)
        sum_ref[...] = jnp.zeros((16, 128), F32)

        def half_of(base, far_refs):
            def rows_of(i, carry):
                inner = pl.ds(pl.multiple_of(i * tile, tile), tile)
                rows = pl.ds(pl.multiple_of(base + i * tile, tile), tile)
                products = total_ref[rows, : 2 * rank]
                squares = total_ref[rows, 2 * rank :]
                for k, ref in enumerate(far_refs):
                    block = ref[inner, :]
                    products += jnp.dot(block, both_ref[heads[k]], preferred_element_type=F32)
                    wide = block.astype(F32)
                    for c in range(0, columns, 128):
                        squares += wide[:, c : c + 128] * wide[:, c : c + 128]
                latent = products[:, :rank].astype(BF16)
                across = products[:, rank:]
                grad = across
                for k in range(3):
                    grad -= jnp.dot(latent, gram_ref[k], preferred_element_type=F32)
                fit = latent.astype(F32) * (across + grad)
                energy = jnp.sum(squares, axis=1, keepdims=True)
                misfit = energy - jnp.sum(fit, axis=1, keepdims=True)
                own = t_ref[rows, :]
                rest = own.astype(F32) - jnp.dot(latent, u_ref[...], preferred_element_type=F32)
                high = rest.astype(BF16)
                low = (rest - high.astype(F32)).astype(BF16)
                upg_ref[...] += lax.dot_general(latent, high, tn, preferred_element_type=F32) + lax.dot_general(
                    latent, low, tn, preferred_element_type=F32
                )
                down_ref[...] += lax.dot_general(grad.astype(BF16), own, tn, preferred_element_type=F32)
                lane = lax.broadcasted_iota(jnp.int32, (1, 128), 1)
                sum_ref[0:1, :] += jnp.where(lane == 0, jnp.sum(energy), jnp.where(lane == 1, jnp.sum(misfit), 0.0))
                return carry

            lax.fori_loop(0, half // tile, rows_of, 0)

        half_of(0, (far0, far2))
        half_of(half, (far1, far3))
        lane = lax.broadcasted_iota(jnp.int32, (1, 128), 1)
        energy = jnp.sum(jnp.where(lane == 0, sum_ref[0:1, :], 0.0))
        misfit = jnp.sum(jnp.where(lane == 1, sum_ref[0:1, :], 0.0))
        tail = spread(lax.broadcasted_iota(jnp.int32, (rows_out, 128), 1), energy, misfit).astype(BF16)
        for s in range(SEQ):
            rows = slice(s * rows_out, (s + 1) * rows_out)
            out_ref[s, :, 0:columns] = down_ref[rows, :].astype(BF16)
            out_ref[s, :, columns : 2 * columns] = upg_ref[rows, :].astype(BF16)
            out_ref[s, :, 2 * columns :] = tail

    whole = pl.BlockSpec(memory_space=pltpu.VMEM)
    return pl.pallas_call(
        kernel,
        out_shape=jax.ShapeDtypeStruct((SEQ, rows_out, 2 * columns + 128), BF16),
        in_specs=[whole] * 9,
        out_specs=whole,
        scratch_shapes=[
            pltpu.VMEM((rank, columns), F32),
            pltpu.VMEM((rank, columns), F32),
            pltpu.VMEM((16, 128), F32),
        ],
        compiler_params=pltpu.CompilerParams(vmem_limit_bytes=24 * MIB),
    )(both, *far, total, gram, targets, up)


def finish(parts, columns, tokens_all):
    blocks, rows, width = parts.shape
    entries = tokens_all * 2 * KEY_VALUE_HEADS * HEAD_SIZE

    def kernel(p_ref, down_ref, up_ref, rel_ref):
        total = jnp.zeros((rows, width), F32)
        for s in range(blocks):
            total += p_ref[s].astype(F32)
        tail = total[0:1, 2 * columns :]
        lane = lax.broadcasted_iota(jnp.int32, tail.shape, 1)
        energy = jnp.sum(jnp.where(lane < 3, tail, 0.0), keepdims=True)
        misfit = jnp.sum(jnp.where((lane >= 3) & (lane < 6), tail, 0.0), keepdims=True)
        factor = -(entries / energy) / math.sqrt(tokens_all)
        down_ref[...] = total[:, :columns] * factor
        up_ref[...] = total[:, columns : 2 * columns] * factor
        rel_ref[...] = misfit / energy

    whole = pl.BlockSpec(memory_space=pltpu.VMEM)
    return pl.pallas_call(
        kernel,
        out_shape=[
            jax.ShapeDtypeStruct((rows, columns), F32),
            jax.ShapeDtypeStruct((rows, columns), F32),
            jax.ShapeDtypeStruct((1, 1), F32),
        ],
        in_specs=[whole],
        out_specs=[whole] * 3,
        compiler_params=pltpu.CompilerParams(vmem_limit_bytes=4 * MIB),
    )(parts)


def per_device(hidden, key_value_weight, down_projection, up_projection, positions):
    rows_here = hidden.shape[0]
    tokens_all = lax.axis_size("seq") * rows_here
    both = lax.all_gather(head_factors(down_projection, up_projection), "head", axis=0)
    half_dim = HEAD_SIZE // 2
    freqs = jnp.power(F32(THETA), -(jnp.arange(half_dim, dtype=F32) * 2.0 / HEAD_SIZE))
    angle = positions.astype(F32)[:, None] * freqs[None, :]
    cosine, sine = jnp.cos(angle), jnp.sin(angle)
    cosine = jnp.concatenate([cosine, cosine], axis=1)
    sine = jnp.concatenate([-sine, sine], axis=1)
    targets = None
    groups = gather_weight(key_value_weight)
    for i, group in enumerate(groups):
        last = i == len(groups) - 1
        targets = dense_step(hidden, group, targets, (cosine, sine) if last else None)
    half = rows_here // 2
    swap = [(h, h ^ 1) for h in range(HEADS)]
    targets, both = lax.optimization_barrier((targets, both))
    below = lax.ppermute(targets, "head", y_shift(1))
    above = lax.ppermute(targets, "head", y_shift(-1))
    partner = lax.ppermute(targets, "head", swap)
    total, gram = head_products((0,), both, [targets, partner], None)
    below, above, total = lax.optimization_barrier((below, above, total))
    far = [lax.ppermute(below[:half], "head", y_shift(1)), lax.ppermute(above[half:], "head", y_shift(-1))]
    pieces = [below, lax.ppermute(below, "head", swap), above, lax.ppermute(above, "head", swap)]
    (total,) = head_products((-1, 1), both, pieces, total)
    *far, total = lax.optimization_barrier((*far, total))
    far += [lax.ppermute(rows, "head", swap) for rows in far]
    parts = factor_grads(both, far, total, gram, targets, up_projection)
    parts = lax.all_to_all(parts, "seq", 0, 0)
    grad_down, grad_up, rel_error = finish(parts, HEAD_COLUMNS, tokens_all)
    return grad_down, grad_up, rel_error.reshape(())


def solution(mesh):
    return jax.shard_map(
        per_device,
        mesh=mesh,
        in_specs=(P("seq", None), P("seq", "head"), P("head", None), P(None, "head"), P("seq")),
        out_specs=(P("seq", "head"), P("seq", "head"), P()),
        check_vma=False,
    )
```

```python
import math

import jax
import jax.numpy as jnp
from jax import lax
from jax.experimental import pallas as pl
from jax.experimental.pallas import tpu as pltpu
from jax.sharding import PartitionSpec as P

KEY_VALUE_HEADS = 8
HEAD_SIZE = 128
HEAD_COLUMNS = 2 * HEAD_SIZE
LATENT_RANK = 512
THETA = 500000.0
X, Y, Z, HEADS = 4, 4, 8, 8
SEQ = X * Z
MIB = 1024 * 1024
F32 = jnp.float32
BF16 = jnp.bfloat16


def z_shift(k):
    return [(x * Z + z, x * Z + (z + k) % Z) for x in range(X) for z in range(Z)]


def x_shift(k):
    return [(x * Z + z, ((x + k) % X) * Z + z) for x in range(X) for z in range(Z)]


def y_shift(k):
    return [(y * 2 + c, ((y + k) % Y) * 2 + c) for y in range(Y) for c in range(2)]


def head_swap():
    return [(h, h ^ 1) for h in range(HEADS)]


def both_ways(up, down, axis, shift):
    return lax.ppermute(up, axis, shift(1)), lax.ppermute(down, axis, shift(-1))


def halves(up, down, axis, shift):
    half = up.shape[0] // 2
    return both_ways(up[:half], down[half:], axis, shift)


def gather(weight, down, up):
    ordered = lax.optimization_barrier
    own = head_factors(down, up)
    weight, own = ordered((weight, own))
    part_rows = weight.shape[0] // 2
    part_a, part_b = weight[:part_rows], weight[part_rows:]
    b_order, a_order = [0, -1, 1, 2], [0, -1, 1, -2, 2, -3, 3, 4]
    b_near = both_ways(part_b, part_b, "seq", x_shift)
    b_far = lax.ppermute(part_b, "seq", x_shift(X // 2))
    a_near = both_ways(part_a, part_a, "seq", z_shift)
    b_all = jnp.concatenate([part_b, *b_near, b_far], axis=0)
    factors = [own]
    for _ in range(Y - 1):
        factors.append(lax.ppermute(factors[-1], "head", y_shift(1)))
    b_rounds = [both_ways(b_all, b_all, "seq", z_shift)]
    for _ in range(2):
        b_rounds.append(both_ways(*b_rounds[-1], "seq", z_shift))
    b_last = halves(*b_rounds[-1], "seq", z_shift)
    a_rounds = [a_near]
    for _ in range(2):
        a_rounds.append(both_ways(*a_rounds[-1], "seq", z_shift))
    a_end = halves(*a_rounds[-1], "seq", z_shift)
    a_all = jnp.concatenate([part_a, *(rows for pair in a_rounds for rows in pair), *a_end], axis=0)
    a_x = ordered(both_ways(a_all, a_all, "seq", x_shift))
    a_last = halves(*a_x, "seq", x_shift)

    def column(dx):
        return [(dx, dz, 0) for dz in a_order]

    def row(dz):
        return [(dx, dz, 1) for dx in b_order]

    pieces = [(b_all, row(0)), (a_all, column(0)), (a_x[0], column(-1)), (a_x[1], column(1))]
    for k, blocks in enumerate(b_rounds):
        pieces += [(blocks[0], row(-k - 1)), (blocks[1], row(k + 1))]
    last = [(a_last[0], column(X // 2)[: Z // 2]), (a_last[1], column(X // 2)[Z // 2 :])]
    last += [(b_last[0], row(Z // 2)[: X // 2]), (b_last[1], row(Z // 2)[X // 2 :])]
    return pieces, last, factors


def column_of(entry):
    dx, dz, part = entry
    here = lax.axis_index("seq")
    owner = ((here // Z + dx + X) % X) * Z + (here % Z + dz + Z) % Z
    return pl.multiple_of(owner * 256 + part * 128, 128)


def dense_most(hidden, pieces, last):
    rows, width = hidden.shape
    columns = pieces[0][0].shape[1]
    missing = [entry for _, entries in last for entry in entries]
    chunk, tile = 128, 256
    chunks = rows // chunk

    def kernel(hidden_ref, *rest):
        piece_refs, (out_ref, far_ref, block_ref, weight_ref, sems, far_sems) = rest[: len(pieces)], rest[len(pieces) :]
        copies = [
            pltpu.make_async_copy(
                hidden_ref.at[i * chunk : (i + 1) * chunk, :], block_ref.at[i * chunk : (i + 1) * chunk, :], sems.at[i]
            )
            for i in range(chunks)
        ]
        far_copies = [
            pltpu.make_async_copy(
                hidden_ref.at[:, pl.ds(column_of(entry), 128)], far_ref.at[:, i * 128 : (i + 1) * 128], far_sems.at[i]
            )
            for i, entry in enumerate(missing)
        ]
        for copy in copies + far_copies:
            copy.start()
        for entry in missing:
            weight_ref[pl.ds(column_of(entry), 128), :] = jnp.zeros((128, columns), BF16)
        for ref, (_, entries) in zip(piece_refs, pieces):
            for i, entry in enumerate(entries):
                weight_ref[pl.ds(column_of(entry), 128), :] = ref[i * 128 : (i + 1) * 128, :]
        for row in range(0, rows, tile):
            for copy in copies[row // chunk : (row + tile) // chunk]:
                copy.wait()
            out_ref[row : row + tile, :] = jnp.dot(
                block_ref[row : row + tile, :], weight_ref[...], preferred_element_type=F32
            )
        for copy in far_copies:
            copy.wait()

    whole = pl.BlockSpec(memory_space=pltpu.VMEM)
    return pl.pallas_call(
        kernel,
        out_shape=[
            jax.ShapeDtypeStruct((rows, columns), F32),
            jax.ShapeDtypeStruct((rows, 128 * len(missing)), BF16),
        ],
        in_specs=[pl.BlockSpec(memory_space=pltpu.HBM)] + [whole] * len(pieces),
        out_specs=[whole] * 2,
        scratch_shapes=[
            pltpu.VMEM((rows, width), BF16),
            pltpu.VMEM((width, columns), BF16),
            pltpu.SemaphoreType.DMA((chunks,)),
            pltpu.SemaphoreType.DMA((len(missing),)),
        ],
        compiler_params=pltpu.CompilerParams(vmem_limit_bytes=44 * MIB),
        cost_estimate=pl.CostEstimate(
            flops=2 * rows * width * columns, bytes_accessed=2 * rows * width, transcendentals=0
        ),
    )(hidden, *[rows_ for rows_, _ in pieces])


def dense_last(far, total, last, cosine, sine):
    rows, columns = total.shape

    def kernel(far_ref, total_ref, cos_ref, sin_ref, *rest):
        piece_refs, out_ref = rest[:-1], rest[-1]
        tile = 256
        for row in range(0, rows, tile):
            here = slice(row, row + tile)
            dense = total_ref[here, :]
            start = 0
            for ref in piece_refs:
                depth = ref.shape[0]
                dense += jnp.dot(far_ref[here, start : start + depth], ref[...], preferred_element_type=F32)
                start += depth
            keys = dense[:, :HEAD_SIZE]
            turned = keys * cos_ref[here, :] + pltpu.roll(keys, HEAD_SIZE // 2, 1) * sin_ref[here, :]
            out_ref[here, :HEAD_SIZE] = turned.astype(BF16)
            out_ref[here, HEAD_SIZE:] = dense[:, HEAD_SIZE:].astype(BF16)

    whole = pl.BlockSpec(memory_space=pltpu.VMEM)
    return pl.pallas_call(
        kernel,
        out_shape=jax.ShapeDtypeStruct((rows, columns), BF16),
        in_specs=[whole] * (4 + len(last)),
        out_specs=whole,
        compiler_params=pltpu.CompilerParams(vmem_limit_bytes=16 * MIB),
    )(far, total, cosine, sine, *[rows_ for rows_, _ in last])


def split3(value):
    high = value.astype(BF16).astype(F32)
    middle = (value - high).astype(BF16).astype(F32)
    return high, middle, value - high - middle


def spread(lane, first, second):
    out = jnp.zeros(lane.shape, F32)
    for i, part in enumerate((*split3(first), *split3(second))):
        out = jnp.where(lane == i, part, out)
    return out


def head_factors(down, up):
    columns, rank = down.shape

    def kernel(d_ref, u_ref, out_ref):
        out_ref[:, :rank] = d_ref[...]
        out_ref[:, rank:] = u_ref[...].astype(F32).T.astype(BF16)

    whole = pl.BlockSpec(memory_space=pltpu.VMEM)
    return pl.pallas_call(
        kernel,
        out_shape=jax.ShapeDtypeStruct((columns, 2 * rank), BF16),
        in_specs=[whole] * 2,
        out_specs=whole,
        compiler_params=pltpu.CompilerParams(vmem_limit_bytes=4 * MIB),
    )(down, up)


def gram_terms(joined, swapped):
    rank = joined.shape[1] // 2

    def kernel(joined_ref, swapped_ref, out_ref):
        gram = jnp.zeros((rank, rank), F32)
        for ref in (joined_ref, swapped_ref):
            part = ref[:, rank:]
            gram += lax.dot_general(part, part, (((0,), (0,)), ((), ())), preferred_element_type=F32)
        high = gram.astype(BF16)
        out_ref[0] = high
        out_ref[1] = (gram - high.astype(F32)).astype(BF16)

    whole = pl.BlockSpec(memory_space=pltpu.VMEM)
    return pl.pallas_call(
        kernel,
        out_shape=jax.ShapeDtypeStruct((2, rank, rank), BF16),
        in_specs=[whole] * 2,
        out_specs=whole,
        compiler_params=pltpu.CompilerParams(vmem_limit_bytes=16 * MIB),
    )(joined, swapped)


def head_products(pieces, joined, swapped, chips, total):
    tokens, columns = pieces[0].shape
    rank = joined.shape[1] // 2
    count = len(pieces)
    extra = [] if total is None else [total]

    def kernel(*refs):
        piece_refs, factor_refs, extra_refs, out_ref = refs[:count], refs[count : count + 2], refs[count + 2 : -1], refs[-1]
        tile = 256

        def rows_of(i, carry):
            rows = pl.ds(pl.multiple_of(i * tile, tile), tile)
            products = extra_refs[0][rows, : 2 * rank] if extra else jnp.zeros((tile, 2 * rank), F32)
            squares = extra_refs[0][rows, 2 * rank :] if extra else jnp.zeros((tile, 128), F32)
            for k, ref in enumerate(piece_refs):
                block = ref[rows, :]
                chip = chips[k // 2]
                factor = factor_refs[k % 2][chip * columns : (chip + 1) * columns, :]
                products += jnp.dot(block, factor, preferred_element_type=F32)
                wide = block.astype(F32)
                for c in range(0, columns, 128):
                    squares += wide[:, c : c + 128] * wide[:, c : c + 128]
            out_ref[rows, : 2 * rank] = products
            out_ref[rows, 2 * rank :] = squares
            return carry

        lax.fori_loop(0, tokens // tile, rows_of, 0)

    whole = pl.BlockSpec(memory_space=pltpu.VMEM)
    return pl.pallas_call(
        kernel,
        out_shape=jax.ShapeDtypeStruct((tokens, 2 * rank + 128), F32),
        in_specs=[whole] * (count + 2 + len(extra)),
        out_specs=whole,
        compiler_params=pltpu.CompilerParams(vmem_limit_bytes=24 * MIB),
        cost_estimate=pl.CostEstimate(
            flops=4 * tokens * columns * rank * count, bytes_accessed=2 * tokens * columns, transcendentals=0
        ),
    )(*pieces, joined, swapped, *extra)


def factor_grads(far, joined, swapped, total, gram, targets, up):
    tokens, columns = targets.shape
    rank = up.shape[0]
    rows_out = rank // SEQ
    half = tokens // 2
    tn = (((0,), (0,)), ((), ()))

    def kernel(far0, far1, far2, far3, factor0, factor1, total_ref, gram_ref, t_ref, u_ref, out_ref, down_ref, upg_ref, sum_ref):
        tile = 256
        down_ref[...] = jnp.zeros((rank, columns), F32)
        upg_ref[...] = jnp.zeros((rank, columns), F32)
        sum_ref[...] = jnp.zeros((16, 128), F32)

        def half_of(base, far_refs):
            def rows_of(i, carry):
                inner = pl.ds(pl.multiple_of(i * tile, tile), tile)
                rows = pl.ds(pl.multiple_of(base + i * tile, tile), tile)
                products = total_ref[rows, : 2 * rank]
                squares = total_ref[rows, 2 * rank :]
                for ref, factor_ref in zip(far_refs, (factor0, factor1)):
                    block = ref[inner, :]
                    factor = factor_ref[2 * columns : 3 * columns, :]
                    products += jnp.dot(block, factor, preferred_element_type=F32)
                    wide = block.astype(F32)
                    for c in range(0, columns, 128):
                        squares += wide[:, c : c + 128] * wide[:, c : c + 128]
                latent = products[:, :rank].astype(BF16)
                across = products[:, rank:]
                grad = across
                for k in range(2):
                    grad -= jnp.dot(latent, gram_ref[k], preferred_element_type=F32)
                fit = latent.astype(F32) * (across + grad)
                energy = jnp.sum(squares, axis=1, keepdims=True)
                misfit = energy - jnp.sum(fit, axis=1, keepdims=True)
                own = t_ref[rows, :]
                rest = own.astype(F32) - jnp.dot(latent, u_ref[...], preferred_element_type=F32)
                high = rest.astype(BF16)
                low = (rest - high.astype(F32)).astype(BF16)
                upg_ref[...] += lax.dot_general(latent, high, tn, preferred_element_type=F32) + lax.dot_general(
                    latent, low, tn, preferred_element_type=F32
                )
                down_ref[...] += lax.dot_general(grad.astype(BF16), own, tn, preferred_element_type=F32)
                lane = lax.broadcasted_iota(jnp.int32, (1, 128), 1)
                sum_ref[0:1, :] += jnp.where(lane == 0, jnp.sum(energy), jnp.where(lane == 1, jnp.sum(misfit), 0.0))
                return carry

            lax.fori_loop(0, half // tile, rows_of, 0)

        half_of(0, (far0, far2))
        half_of(half, (far1, far3))
        lane = lax.broadcasted_iota(jnp.int32, (1, 128), 1)
        energy = jnp.sum(jnp.where(lane == 0, sum_ref[0:1, :], 0.0))
        misfit = jnp.sum(jnp.where(lane == 1, sum_ref[0:1, :], 0.0))
        tail = spread(lax.broadcasted_iota(jnp.int32, (rows_out, 128), 1), energy, misfit).astype(BF16)
        for s in range(SEQ):
            rows = slice(s * rows_out, (s + 1) * rows_out)
            out_ref[s, :, 0:columns] = down_ref[rows, :].astype(BF16)
            out_ref[s, :, columns : 2 * columns] = upg_ref[rows, :].astype(BF16)
            out_ref[s, :, 2 * columns :] = tail

    whole = pl.BlockSpec(memory_space=pltpu.VMEM)
    return pl.pallas_call(
        kernel,
        out_shape=jax.ShapeDtypeStruct((SEQ, rows_out, 2 * columns + 128), BF16),
        in_specs=[whole] * 10,
        out_specs=whole,
        scratch_shapes=[
            pltpu.VMEM((rank, columns), F32),
            pltpu.VMEM((rank, columns), F32),
            pltpu.VMEM((16, 128), F32),
        ],
        compiler_params=pltpu.CompilerParams(vmem_limit_bytes=24 * MIB),
    )(*far, joined, swapped, total, gram, targets, up)


def finish(parts, columns, tokens_all):
    blocks, rows, width = parts.shape
    entries = tokens_all * 2 * KEY_VALUE_HEADS * HEAD_SIZE

    def kernel(p_ref, down_ref, up_ref, rel_ref):
        total = jnp.zeros((rows, width), F32)
        for s in range(blocks):
            total += p_ref[s].astype(F32)
        tail = total[0:1, 2 * columns :]
        lane = lax.broadcasted_iota(jnp.int32, tail.shape, 1)
        energy = jnp.sum(jnp.where(lane < 3, tail, 0.0), keepdims=True)
        misfit = jnp.sum(jnp.where((lane >= 3) & (lane < 6), tail, 0.0), keepdims=True)
        factor = -(entries / energy) / math.sqrt(tokens_all)
        down_ref[...] = total[:, :columns] * factor
        up_ref[...] = total[:, columns : 2 * columns] * factor
        rel_ref[...] = misfit / energy

    whole = pl.BlockSpec(memory_space=pltpu.VMEM)
    return pl.pallas_call(
        kernel,
        out_shape=[
            jax.ShapeDtypeStruct((rows, columns), F32),
            jax.ShapeDtypeStruct((rows, columns), F32),
            jax.ShapeDtypeStruct((1, 1), F32),
        ],
        in_specs=[whole],
        out_specs=[whole] * 3,
        compiler_params=pltpu.CompilerParams(vmem_limit_bytes=4 * MIB),
    )(parts)


def per_device(hidden, key_value_weight, down_projection, up_projection, positions):
    rows_here = hidden.shape[0]
    tokens_all = lax.axis_size("seq") * rows_here
    swap = head_swap()
    pieces, last, factors = gather(key_value_weight, down_projection, up_projection)
    half_dim = HEAD_SIZE // 2
    freqs = jnp.power(F32(THETA), -(jnp.arange(half_dim, dtype=F32) * 2.0 / HEAD_SIZE))
    angle = positions.astype(F32)[:, None] * freqs[None, :]
    cosine, sine = jnp.cos(angle), jnp.sin(angle)
    cosine = jnp.concatenate([cosine, cosine], axis=1)
    sine = jnp.concatenate([-sine, sine], axis=1)
    total, far_columns = dense_most(hidden, pieces, last)
    ordered = lax.optimization_barrier
    columns = factors[0].shape[0]
    total, *factors = ordered((total, *factors))
    joined = jnp.concatenate(factors, axis=0)
    targets = dense_last(far_columns, total, last, cosine, sine)
    targets, joined = ordered((targets, joined))
    half = rows_here // 2
    below = lax.ppermute(targets, "head", y_shift(1))
    above = lax.ppermute(targets, "head", y_shift(-1))
    partner = lax.ppermute(targets, "head", swap)
    swapped = lax.ppermute(joined, "head", swap)
    total = head_products([targets, partner], joined, swapped, (0,), None)
    below, above, total = ordered((below, above, total))
    far = [lax.ppermute(below[:half], "head", y_shift(1)), lax.ppermute(above[half:], "head", y_shift(-1))]
    pieces = [below, lax.ppermute(below, "head", swap), above, lax.ppermute(above, "head", swap)]
    total = head_products(pieces, joined, swapped, (1, 3), total)
    gram = gram_terms(joined, swapped)
    *far, total, gram = ordered((*far, total, gram))
    far += [lax.ppermute(rows, "head", swap) for rows in far]
    parts = factor_grads(far, joined, swapped, total, gram, targets, up_projection)
    parts = lax.all_to_all(parts, "seq", 0, 0)
    grad_down, grad_up, rel_error = finish(parts, HEAD_COLUMNS, tokens_all)
    return grad_down, grad_up, rel_error.reshape(())


def solution(mesh):
    return jax.shard_map(
        per_device,
        mesh=mesh,
        in_specs=(P("seq", None), P("seq", "head"), P("head", None), P(None, "head"), P("seq")),
        out_specs=(P("seq", "head"), P("seq", "head"), P()),
        check_vma=False,
    )
```

```python
import math

import jax
import jax.numpy as jnp
from jax import lax
from jax.experimental import pallas as pl
from jax.experimental.pallas import tpu as pltpu
from jax.sharding import PartitionSpec as P

KEY_VALUE_HEADS = 8
HEAD_SIZE = 128
HEAD_COLUMNS = 2 * HEAD_SIZE
LATENT_RANK = 512
THETA = 500000.0
X, Y, Z, HEADS = 4, 4, 8, 8
SEQ = X * Z
MIB = 1024 * 1024
F32 = jnp.float32
BF16 = jnp.bfloat16


def z_shift(k):
    return [(x * Z + z, x * Z + (z + k) % Z) for x in range(X) for z in range(Z)]


def x_shift(k):
    return [(x * Z + z, ((x + k) % X) * Z + z) for x in range(X) for z in range(Z)]


def y_shift(k):
    return [(y * 2 + c, ((y + k) % Y) * 2 + c) for y in range(Y) for c in range(2)]


def head_swap():
    return [(h, h ^ 1) for h in range(HEADS)]


def both_ways(up, down, axis, shift):
    return lax.ppermute(up, axis, shift(1)), lax.ppermute(down, axis, shift(-1))


def halves(up, down, axis, shift):
    half = up.shape[0] // 2
    return both_ways(up[:half], down[half:], axis, shift)


def gather(weight, down, up):
    ordered = lax.optimization_barrier
    own = head_factors(down, up)
    weight, own = ordered((weight, own))
    part_rows = weight.shape[0] // 2
    part_a, part_b = weight[:part_rows], weight[part_rows:]
    b_order, a_order = [0, -1, 1, 2], [0, -1, 1, -2, 2, -3, 3, 4]
    b_near = both_ways(part_b, part_b, "seq", x_shift)
    b_far = lax.ppermute(part_b, "seq", x_shift(X // 2))
    a_near = both_ways(part_a, part_a, "seq", z_shift)
    b_all = jnp.concatenate([part_b, *b_near, b_far], axis=0)
    factors = [own]
    for _ in range(Y - 1):
        factors.append(lax.ppermute(factors[-1], "head", y_shift(1)))
    b_rounds = [both_ways(b_all, b_all, "seq", z_shift)]
    for _ in range(2):
        b_rounds.append(both_ways(*b_rounds[-1], "seq", z_shift))
    b_last = halves(*b_rounds[-1], "seq", z_shift)
    a_rounds = [a_near]
    for _ in range(2):
        a_rounds.append(both_ways(*a_rounds[-1], "seq", z_shift))
    a_end = halves(*a_rounds[-1], "seq", z_shift)
    a_all = jnp.concatenate([part_a, *(rows for pair in a_rounds for rows in pair), *a_end], axis=0)
    a_x = ordered(both_ways(a_all, a_all, "seq", x_shift))
    a_last = halves(*a_x, "seq", x_shift)

    def column(dx):
        return [(dx, dz, 0) for dz in a_order]

    def row(dz):
        return [(dx, dz, 1) for dx in b_order]

    pieces = [(b_all, row(0)), (a_all, column(0)), (a_x[0], column(-1)), (a_x[1], column(1))]
    for k, blocks in enumerate(b_rounds):
        pieces += [(blocks[0], row(-k - 1)), (blocks[1], row(k + 1))]
    last = [(a_last[0], column(X // 2)[: Z // 2]), (a_last[1], column(X // 2)[Z // 2 :])]
    last += [(b_last[0], row(Z // 2)[: X // 2]), (b_last[1], row(Z // 2)[X // 2 :])]
    return pieces, last, factors


def column_of(entry):
    dx, dz, part = entry
    here = lax.axis_index("seq")
    owner = ((here // Z + dx + X) % X) * Z + (here % Z + dz + Z) % Z
    return pl.multiple_of(owner * 256 + part * 128, 128)


def dense_most(hidden, pieces, last):
    rows, width = hidden.shape
    columns = pieces[0][0].shape[1]
    missing = [entry for _, entries in last for entry in entries]
    chunk, tile = 128, 256
    chunks = rows // chunk

    def kernel(hidden_ref, *rest):
        piece_refs, (out_ref, far_ref, block_ref, weight_ref, sems) = rest[: len(pieces)], rest[len(pieces) :]
        copies = [
            pltpu.make_async_copy(
                hidden_ref.at[i * chunk : (i + 1) * chunk, :], block_ref.at[i * chunk : (i + 1) * chunk, :], sems.at[i]
            )
            for i in range(chunks)
        ]
        ahead = 3
        for copy in copies[:ahead]:
            copy.start()
        for entry in missing:
            weight_ref[pl.ds(column_of(entry), 128), :] = jnp.zeros((128, columns), BF16)
        for ref, (_, entries) in zip(piece_refs, pieces):
            for i, entry in enumerate(entries):
                weight_ref[pl.ds(column_of(entry), 128), :] = ref[i * 128 : (i + 1) * 128, :]
        for row in range(0, rows, tile):
            here = slice(row, row + tile)
            for i in range(row // chunk, (row + tile) // chunk):
                copies[i].wait()
                if i + ahead < chunks:
                    copies[i + ahead].start()
            out_ref[here, :] = jnp.dot(block_ref[here, :], weight_ref[...], preferred_element_type=F32)
            for i, entry in enumerate(missing):
                far_ref[here, i * 128 : (i + 1) * 128] = block_ref[here, pl.ds(column_of(entry), 128)]

    whole = pl.BlockSpec(memory_space=pltpu.VMEM)
    return pl.pallas_call(
        kernel,
        out_shape=[
            jax.ShapeDtypeStruct((rows, columns), F32),
            jax.ShapeDtypeStruct((rows, 128 * len(missing)), BF16),
        ],
        in_specs=[pl.BlockSpec(memory_space=pltpu.HBM)] + [whole] * len(pieces),
        out_specs=[whole] * 2,
        scratch_shapes=[
            pltpu.VMEM((rows, width), BF16),
            pltpu.VMEM((width, columns), BF16),
            pltpu.SemaphoreType.DMA((chunks,)),
        ],
        compiler_params=pltpu.CompilerParams(vmem_limit_bytes=44 * MIB),
        cost_estimate=pl.CostEstimate(
            flops=2 * rows * width * columns, bytes_accessed=2 * rows * width, transcendentals=0
        ),
    )(hidden, *[rows_ for rows_, _ in pieces])


def dense_last(far, total, last, cosine, sine):
    rows, columns = total.shape

    def kernel(far_ref, total_ref, cos_ref, sin_ref, *rest):
        piece_refs, out_ref = rest[:-1], rest[-1]
        tile = 256
        for row in range(0, rows, tile):
            here = slice(row, row + tile)
            dense = total_ref[here, :]
            start = 0
            for ref in piece_refs:
                depth = ref.shape[0]
                dense += jnp.dot(far_ref[here, start : start + depth], ref[...], preferred_element_type=F32)
                start += depth
            keys = dense[:, :HEAD_SIZE]
            turned = keys * cos_ref[here, :] + pltpu.roll(keys, HEAD_SIZE // 2, 1) * sin_ref[here, :]
            out_ref[here, :HEAD_SIZE] = turned.astype(BF16)
            out_ref[here, HEAD_SIZE:] = dense[:, HEAD_SIZE:].astype(BF16)

    whole = pl.BlockSpec(memory_space=pltpu.VMEM)
    return pl.pallas_call(
        kernel,
        out_shape=jax.ShapeDtypeStruct((rows, columns), BF16),
        in_specs=[whole] * (4 + len(last)),
        out_specs=whole,
        compiler_params=pltpu.CompilerParams(vmem_limit_bytes=16 * MIB),
    )(far, total, cosine, sine, *[rows_ for rows_, _ in last])


def split3(value):
    high = value.astype(BF16).astype(F32)
    middle = (value - high).astype(BF16).astype(F32)
    return high, middle, value - high - middle


def spread(lane, first, second):
    out = jnp.zeros(lane.shape, F32)
    for i, part in enumerate((*split3(first), *split3(second))):
        out = jnp.where(lane == i, part, out)
    return out


def head_factors(down, up):
    columns, rank = down.shape

    def kernel(d_ref, u_ref, out_ref):
        out_ref[:, :rank] = d_ref[...]
        out_ref[:, rank:] = u_ref[...].astype(F32).T.astype(BF16)

    whole = pl.BlockSpec(memory_space=pltpu.VMEM)
    return pl.pallas_call(
        kernel,
        out_shape=jax.ShapeDtypeStruct((columns, 2 * rank), BF16),
        in_specs=[whole] * 2,
        out_specs=whole,
        compiler_params=pltpu.CompilerParams(vmem_limit_bytes=4 * MIB),
    )(down, up)


def gram_terms(joined, swapped):
    rank = joined.shape[1] // 2

    def kernel(joined_ref, swapped_ref, out_ref):
        gram = jnp.zeros((rank, rank), F32)
        for ref in (joined_ref, swapped_ref):
            part = ref[:, rank:]
            gram += lax.dot_general(part, part, (((0,), (0,)), ((), ())), preferred_element_type=F32)
        high = gram.astype(BF16)
        out_ref[0] = high
        out_ref[1] = (gram - high.astype(F32)).astype(BF16)

    whole = pl.BlockSpec(memory_space=pltpu.VMEM)
    return pl.pallas_call(
        kernel,
        out_shape=jax.ShapeDtypeStruct((2, rank, rank), BF16),
        in_specs=[whole] * 2,
        out_specs=whole,
        compiler_params=pltpu.CompilerParams(vmem_limit_bytes=16 * MIB),
    )(joined, swapped)


def head_products(pieces, joined, swapped, chips, total):
    tokens, columns = pieces[0].shape
    rank = joined.shape[1] // 2
    count = len(pieces)
    extra = [] if total is None else [total]

    def kernel(*refs):
        piece_refs, factor_refs, extra_refs, out_ref = refs[:count], refs[count : count + 2], refs[count + 2 : -1], refs[-1]
        tile = 256

        def rows_of(i, carry):
            rows = pl.ds(pl.multiple_of(i * tile, tile), tile)
            products = extra_refs[0][rows, : 2 * rank] if extra else jnp.zeros((tile, 2 * rank), F32)
            squares = extra_refs[0][rows, 2 * rank :] if extra else jnp.zeros((tile, 128), F32)
            for k, ref in enumerate(piece_refs):
                block = ref[rows, :]
                chip = chips[k // 2]
                factor = factor_refs[k % 2][chip * columns : (chip + 1) * columns, :]
                products += jnp.dot(block, factor, preferred_element_type=F32)
                wide = block.astype(F32)
                for c in range(0, columns, 128):
                    squares += wide[:, c : c + 128] * wide[:, c : c + 128]
            out_ref[rows, : 2 * rank] = products
            out_ref[rows, 2 * rank :] = squares
            return carry

        lax.fori_loop(0, tokens // tile, rows_of, 0)

    whole = pl.BlockSpec(memory_space=pltpu.VMEM)
    return pl.pallas_call(
        kernel,
        out_shape=jax.ShapeDtypeStruct((tokens, 2 * rank + 128), F32),
        in_specs=[whole] * (count + 2 + len(extra)),
        out_specs=whole,
        compiler_params=pltpu.CompilerParams(vmem_limit_bytes=24 * MIB),
        cost_estimate=pl.CostEstimate(
            flops=4 * tokens * columns * rank * count, bytes_accessed=2 * tokens * columns, transcendentals=0
        ),
    )(*pieces, joined, swapped, *extra)


def factor_grads(far, joined, swapped, total, gram, targets, up):
    tokens, columns = targets.shape
    rank = up.shape[0]
    rows_out = rank // SEQ
    half = tokens // 2
    tn = (((0,), (0,)), ((), ()))

    def kernel(far0, far1, far2, far3, factor0, factor1, total_ref, gram_ref, t_ref, u_ref, out_ref, down_ref, upg_ref, sum_ref):
        tile = 512
        down_ref[...] = jnp.zeros((rank, columns), F32)
        upg_ref[...] = jnp.zeros((rank, columns), F32)
        sum_ref[...] = jnp.zeros((16, 128), F32)

        def half_of(base, far_refs):
            def rows_of(i, carry):
                inner = pl.ds(pl.multiple_of(i * tile, tile), tile)
                rows = pl.ds(pl.multiple_of(base + i * tile, tile), tile)
                products = total_ref[rows, : 2 * rank]
                squares = total_ref[rows, 2 * rank :]
                for ref, factor_ref in zip(far_refs, (factor0, factor1)):
                    block = ref[inner, :]
                    factor = factor_ref[2 * columns : 3 * columns, :]
                    products += jnp.dot(block, factor, preferred_element_type=F32)
                    wide = block.astype(F32)
                    for c in range(0, columns, 128):
                        squares += wide[:, c : c + 128] * wide[:, c : c + 128]
                latent = products[:, :rank].astype(BF16)
                across = products[:, rank:]
                grad = across
                for k in range(2):
                    grad -= jnp.dot(latent, gram_ref[k], preferred_element_type=F32)
                fit = latent.astype(F32) * (across + grad)
                energy = jnp.sum(squares, axis=1, keepdims=True)
                misfit = energy - jnp.sum(fit, axis=1, keepdims=True)
                own = t_ref[rows, :]
                rest = own.astype(F32) - jnp.dot(latent, u_ref[...], preferred_element_type=F32)
                high = rest.astype(BF16)
                low = (rest - high.astype(F32)).astype(BF16)
                upg_ref[...] += lax.dot_general(latent, high, tn, preferred_element_type=F32) + lax.dot_general(
                    latent, low, tn, preferred_element_type=F32
                )
                down_ref[...] += lax.dot_general(grad.astype(BF16), own, tn, preferred_element_type=F32)
                lane = lax.broadcasted_iota(jnp.int32, (1, 128), 1)
                sum_ref[0:1, :] += jnp.where(lane == 0, jnp.sum(energy), jnp.where(lane == 1, jnp.sum(misfit), 0.0))
                return carry

            lax.fori_loop(0, half // tile, rows_of, 0)

        half_of(0, (far0, far2))
        half_of(half, (far1, far3))
        lane = lax.broadcasted_iota(jnp.int32, (1, 128), 1)
        energy = jnp.sum(jnp.where(lane == 0, sum_ref[0:1, :], 0.0))
        misfit = jnp.sum(jnp.where(lane == 1, sum_ref[0:1, :], 0.0))
        tail = spread(lax.broadcasted_iota(jnp.int32, (rows_out, 128), 1), energy, misfit).astype(BF16)
        for s in range(SEQ):
            rows = slice(s * rows_out, (s + 1) * rows_out)
            out_ref[s, :, 0:columns] = down_ref[rows, :].astype(BF16)
            out_ref[s, :, columns : 2 * columns] = upg_ref[rows, :].astype(BF16)
            out_ref[s, :, 2 * columns :] = tail

    whole = pl.BlockSpec(memory_space=pltpu.VMEM)
    return pl.pallas_call(
        kernel,
        out_shape=jax.ShapeDtypeStruct((SEQ, rows_out, 2 * columns + 128), BF16),
        in_specs=[whole] * 10,
        out_specs=whole,
        scratch_shapes=[
            pltpu.VMEM((rank, columns), F32),
            pltpu.VMEM((rank, columns), F32),
            pltpu.VMEM((16, 128), F32),
        ],
        compiler_params=pltpu.CompilerParams(vmem_limit_bytes=24 * MIB),
    )(*far, joined, swapped, total, gram, targets, up)


def finish(parts, columns, tokens_all):
    blocks, rows, width = parts.shape
    entries = tokens_all * 2 * KEY_VALUE_HEADS * HEAD_SIZE

    def kernel(p_ref, down_ref, up_ref, rel_ref):
        total = jnp.zeros((rows, width), F32)
        for s in range(blocks):
            total += p_ref[s].astype(F32)
        tail = total[0:1, 2 * columns :]
        lane = lax.broadcasted_iota(jnp.int32, tail.shape, 1)
        energy = jnp.sum(jnp.where(lane < 3, tail, 0.0), keepdims=True)
        misfit = jnp.sum(jnp.where((lane >= 3) & (lane < 6), tail, 0.0), keepdims=True)
        factor = -(entries / energy) / math.sqrt(tokens_all)
        down_ref[...] = total[:, :columns] * factor
        up_ref[...] = total[:, columns : 2 * columns] * factor
        rel_ref[...] = misfit / energy

    whole = pl.BlockSpec(memory_space=pltpu.VMEM)
    return pl.pallas_call(
        kernel,
        out_shape=[
            jax.ShapeDtypeStruct((rows, columns), F32),
            jax.ShapeDtypeStruct((rows, columns), F32),
            jax.ShapeDtypeStruct((1, 1), F32),
        ],
        in_specs=[whole],
        out_specs=[whole] * 3,
        compiler_params=pltpu.CompilerParams(vmem_limit_bytes=4 * MIB),
    )(parts)


def per_device(hidden, key_value_weight, down_projection, up_projection, positions):
    rows_here = hidden.shape[0]
    tokens_all = lax.axis_size("seq") * rows_here
    swap = head_swap()
    pieces, last, factors = gather(key_value_weight, down_projection, up_projection)
    half_dim = HEAD_SIZE // 2
    freqs = jnp.power(F32(THETA), -(jnp.arange(half_dim, dtype=F32) * 2.0 / HEAD_SIZE))
    angle = positions.astype(F32)[:, None] * freqs[None, :]
    cosine, sine = jnp.cos(angle), jnp.sin(angle)
    cosine = jnp.concatenate([cosine, cosine], axis=1)
    sine = jnp.concatenate([-sine, sine], axis=1)
    total, far_columns = dense_most(hidden, pieces, last)
    ordered = lax.optimization_barrier
    columns = factors[0].shape[0]
    total, *factors = ordered((total, *factors))
    joined = jnp.concatenate(factors, axis=0)
    targets = dense_last(far_columns, total, last, cosine, sine)
    targets, joined = ordered((targets, joined))
    half = rows_here // 2
    below = lax.ppermute(targets, "head", y_shift(1))
    above = lax.ppermute(targets, "head", y_shift(-1))
    partner = lax.ppermute(targets, "head", swap)
    swapped = lax.ppermute(joined, "head", swap)
    total = head_products([targets, partner], joined, swapped, (0,), None)
    below, above, total = ordered((below, above, total))
    far = [lax.ppermute(below[:half], "head", y_shift(1)), lax.ppermute(above[half:], "head", y_shift(-1))]
    pieces = [below, lax.ppermute(below, "head", swap), above, lax.ppermute(above, "head", swap)]
    total = head_products(pieces, joined, swapped, (1, 3), total)
    gram = gram_terms(joined, swapped)
    *far, total, gram = ordered((*far, total, gram))
    far += [lax.ppermute(rows, "head", swap) for rows in far]
    parts = factor_grads(far, joined, swapped, total, gram, targets, up_projection)
    parts = lax.all_to_all(parts, "seq", 0, 0)
    grad_down, grad_up, rel_error = finish(parts, HEAD_COLUMNS, tokens_all)
    return grad_down, grad_up, rel_error.reshape(())


def solution(mesh):
    return jax.shard_map(
        per_device,
        mesh=mesh,
        in_specs=(P("seq", None), P("seq", "head"), P("head", None), P(None, "head"), P("seq")),
        out_specs=(P("seq", "head"), P("seq", "head"), P()),
        check_vma=False,
    )
```

```python
import math

import jax
import jax.numpy as jnp
from jax import lax
from jax.experimental import pallas as pl
from jax.experimental.pallas import tpu as pltpu
from jax.sharding import PartitionSpec as P

KEY_VALUE_HEADS = 8
HEAD_SIZE = 128
HEAD_COLUMNS = 2 * HEAD_SIZE
LATENT_RANK = 512
THETA = 500000.0
X, Y, Z, HEADS = 4, 4, 8, 8
SEQ = X * Z
MIB = 1024 * 1024
F32 = jnp.float32
BF16 = jnp.bfloat16


def z_shift(k):
    return [(x * Z + z, x * Z + (z + k) % Z) for x in range(X) for z in range(Z)]


def x_shift(k):
    return [(x * Z + z, ((x + k) % X) * Z + z) for x in range(X) for z in range(Z)]


def y_shift(k):
    return [(y * 2 + c, ((y + k) % Y) * 2 + c) for y in range(Y) for c in range(2)]


def head_swap():
    return [(h, h ^ 1) for h in range(HEADS)]


def both_ways(up, down, axis, shift):
    return lax.ppermute(up, axis, shift(1)), lax.ppermute(down, axis, shift(-1))


def halves(up, down, axis, shift):
    half = up.shape[0] // 2
    return both_ways(up[:half], down[half:], axis, shift)


def gather(hidden, weight, down, up, turn):
    ordered = lax.optimization_barrier
    own = head_factors(down, up)
    weight, own = ordered((weight, own))
    part_rows = weight.shape[0] // 2
    part_a, part_b = weight[:part_rows], weight[part_rows:]
    b_order, a_order = [0, -1, 1, 2], [0, -1, 1, -2, 2, -3, 3, 4]

    def column(dx):
        return [(dx, dz, 0) for dz in a_order]

    def row(dz):
        return [(dx, dz, 1) for dx in b_order]

    b_near = both_ways(part_b, part_b, "seq", x_shift)
    b_far = lax.ppermute(part_b, "seq", x_shift(X // 2))
    a_first = both_ways(part_a, part_a, "seq", z_shift)
    b_all = jnp.concatenate([part_b, *b_near, b_far], axis=0)
    factors = [own]
    for _ in range(Y - 1):
        factors.append(lax.ppermute(factors[-1], "head", y_shift(1)))
    b_first = both_ways(b_all, b_all, "seq", z_shift)
    a_second = both_ways(*a_first, "seq", z_shift)
    *a_second, cosine, sine = ordered((*a_second, *turn))
    a_third = both_ways(*a_second, "seq", z_shift)
    pieces = [(b_all, row(0)), (b_first[0], row(-1)), (b_first[1], row(1))]
    (total,) = dense_step(hidden, pieces, None, [])
    *a_third, total = ordered((*a_third, total))
    b_second = both_ways(*b_first, "seq", z_shift)
    a_end = halves(*a_third, "seq", z_shift)
    a_all = jnp.concatenate([part_a, *a_first, *a_second, *a_third, *a_end], axis=0)
    a_x = both_ways(a_all, a_all, "seq", x_shift)
    b_third = both_ways(*b_second, "seq", z_shift)
    (total,) = dense_step(hidden, [(a_all, column(0)), (b_second[0], row(-2)), (b_second[1], row(2))], total, [])
    *a_x, total = ordered((*a_x, total))
    a_last = halves(*a_x, "seq", x_shift)
    b_last = halves(*b_third, "seq", z_shift)
    last = [(a_last[0], column(X // 2)[: Z // 2]), (a_last[1], column(X // 2)[Z // 2 :])]
    last += [(b_last[0], row(Z // 2)[: X // 2]), (b_last[1], row(Z // 2)[X // 2 :])]
    missing = [entry for _, entries in last for entry in entries]
    pieces = [(a_x[0], column(-1)), (a_x[1], column(1)), (b_third[0], row(-3)), (b_third[1], row(3))]
    total, far_columns = dense_step(hidden, pieces, total, missing)
    return total, far_columns, last, factors, (cosine, sine)


def column_of(entry):
    dx, dz, part = entry
    here = lax.axis_index("seq")
    owner = ((here // Z + dx + X) % X) * Z + (here % Z + dz + Z) % Z
    return pl.multiple_of(owner * 256 + part * 128, 128)


def dense_step(hidden, pieces, total, missing):
    rows = hidden.shape[0]
    columns = pieces[0][0].shape[1]
    entries = [entry for _, group in pieces for entry in group]
    count, extra = len(pieces), [] if total is None else [total]

    def kernel(hidden_ref, *refs):
        piece_refs, extra_refs = refs[:count], refs[count : count + len(extra)]
        out_refs, (block_ref, sems) = refs[count + len(extra) : -2], refs[-2:]
        out_ref = out_refs[0]

        def columns_to(entry, to_ref, i, sem):
            return pltpu.make_async_copy(
                hidden_ref.at[:, pl.ds(column_of(entry), 128)], to_ref.at[:, i * 128 : (i + 1) * 128], sems.at[sem]
            )

        copies = [columns_to(entry, block_ref, i, i) for i, entry in enumerate(entries)]
        copies += [columns_to(entry, out_refs[1], i, len(entries) + i) for i, entry in enumerate(missing)]
        for copy in copies:
            copy.start()
        start = 0
        for k, ref in enumerate(piece_refs):
            depth = ref.shape[0]
            for copy in copies[start // 128 : (start + depth) // 128]:
                copy.wait()
            product = jnp.dot(block_ref[:, start : start + depth], ref[...], preferred_element_type=F32)
            if k > 0:
                out_ref[...] += product
            else:
                out_ref[...] = extra_refs[0][...] + product if extra else product
            start += depth
        for copy in copies[len(entries) :]:
            copy.wait()

    whole = pl.BlockSpec(memory_space=pltpu.VMEM)
    out_shape = [jax.ShapeDtypeStruct((rows, columns), F32)]
    if missing:
        out_shape.append(jax.ShapeDtypeStruct((rows, 128 * len(missing)), BF16))
    return pl.pallas_call(
        kernel,
        out_shape=out_shape,
        in_specs=[pl.BlockSpec(memory_space=pltpu.HBM)] + [whole] * (count + len(extra)),
        out_specs=[whole] * len(out_shape),
        scratch_shapes=[
            pltpu.VMEM((rows, 128 * len(entries)), BF16),
            pltpu.SemaphoreType.DMA((len(entries) + len(missing),)),
        ],
        compiler_params=pltpu.CompilerParams(vmem_limit_bytes=44 * MIB),
        cost_estimate=pl.CostEstimate(
            flops=256 * rows * len(entries) * columns, bytes_accessed=256 * rows * len(entries), transcendentals=0
        ),
    )(hidden, *[rows_ for rows_, _ in pieces], *extra)


def dense_last(far, total, last, cosine, sine):
    rows, columns = total.shape

    def kernel(far_ref, total_ref, cos_ref, sin_ref, *rest):
        piece_refs, out_ref = rest[:-1], rest[-1]
        tile = 256
        for row in range(0, rows, tile):
            here = slice(row, row + tile)
            dense = total_ref[here, :]
            start = 0
            for ref in piece_refs:
                depth = ref.shape[0]
                dense += jnp.dot(far_ref[here, start : start + depth], ref[...], preferred_element_type=F32)
                start += depth
            keys = dense[:, :HEAD_SIZE]
            turned = keys * cos_ref[here, :] + pltpu.roll(keys, HEAD_SIZE // 2, 1) * sin_ref[here, :]
            out_ref[here, :HEAD_SIZE] = turned.astype(BF16)
            out_ref[here, HEAD_SIZE:] = dense[:, HEAD_SIZE:].astype(BF16)

    whole = pl.BlockSpec(memory_space=pltpu.VMEM)
    return pl.pallas_call(
        kernel,
        out_shape=jax.ShapeDtypeStruct((rows, columns), BF16),
        in_specs=[whole] * (4 + len(last)),
        out_specs=whole,
        compiler_params=pltpu.CompilerParams(vmem_limit_bytes=16 * MIB),
    )(far, total, cosine, sine, *[rows_ for rows_, _ in last])


def split3(value):
    high = value.astype(BF16).astype(F32)
    middle = (value - high).astype(BF16).astype(F32)
    return high, middle, value - high - middle


def spread(lane, first, second):
    out = jnp.zeros(lane.shape, F32)
    for i, part in enumerate((*split3(first), *split3(second))):
        out = jnp.where(lane == i, part, out)
    return out


def head_factors(down, up):
    columns, rank = down.shape

    def kernel(d_ref, u_ref, out_ref):
        out_ref[:, :rank] = d_ref[...]
        out_ref[:, rank:] = u_ref[...].astype(F32).T.astype(BF16)

    whole = pl.BlockSpec(memory_space=pltpu.VMEM)
    return pl.pallas_call(
        kernel,
        out_shape=jax.ShapeDtypeStruct((columns, 2 * rank), BF16),
        in_specs=[whole] * 2,
        out_specs=whole,
        compiler_params=pltpu.CompilerParams(vmem_limit_bytes=4 * MIB),
    )(down, up)


def gram_terms(joined, swapped):
    rank = joined.shape[1] // 2

    def kernel(joined_ref, swapped_ref, out_ref):
        gram = jnp.zeros((rank, rank), F32)
        for ref in (joined_ref, swapped_ref):
            part = ref[:, rank:]
            gram += lax.dot_general(part, part, (((0,), (0,)), ((), ())), preferred_element_type=F32)
        high = gram.astype(BF16)
        out_ref[0] = high
        out_ref[1] = (gram - high.astype(F32)).astype(BF16)

    whole = pl.BlockSpec(memory_space=pltpu.VMEM)
    return pl.pallas_call(
        kernel,
        out_shape=jax.ShapeDtypeStruct((2, rank, rank), BF16),
        in_specs=[whole] * 2,
        out_specs=whole,
        compiler_params=pltpu.CompilerParams(vmem_limit_bytes=16 * MIB),
    )(joined, swapped)


def head_products(pieces, joined, swapped, chips, total):
    tokens, columns = pieces[0].shape
    rank = joined.shape[1] // 2
    count = len(pieces)
    extra = [] if total is None else [total]

    def kernel(*refs):
        piece_refs, factor_refs, extra_refs, out_ref = refs[:count], refs[count : count + 2], refs[count + 2 : -1], refs[-1]
        tile = 256

        def rows_of(i, carry):
            rows = pl.ds(pl.multiple_of(i * tile, tile), tile)
            products = extra_refs[0][rows, : 2 * rank] if extra else jnp.zeros((tile, 2 * rank), F32)
            squares = extra_refs[0][rows, 2 * rank :] if extra else jnp.zeros((tile, 128), F32)
            for k, ref in enumerate(piece_refs):
                block = ref[rows, :]
                chip = chips[k // 2]
                factor = factor_refs[k % 2][chip * columns : (chip + 1) * columns, :]
                products += jnp.dot(block, factor, preferred_element_type=F32)
                wide = block.astype(F32)
                for c in range(0, columns, 128):
                    squares += wide[:, c : c + 128] * wide[:, c : c + 128]
            out_ref[rows, : 2 * rank] = products
            out_ref[rows, 2 * rank :] = squares
            return carry

        lax.fori_loop(0, tokens // tile, rows_of, 0)

    whole = pl.BlockSpec(memory_space=pltpu.VMEM)
    return pl.pallas_call(
        kernel,
        out_shape=jax.ShapeDtypeStruct((tokens, 2 * rank + 128), F32),
        in_specs=[whole] * (count + 2 + len(extra)),
        out_specs=whole,
        compiler_params=pltpu.CompilerParams(vmem_limit_bytes=24 * MIB),
        cost_estimate=pl.CostEstimate(
            flops=4 * tokens * columns * rank * count, bytes_accessed=2 * tokens * columns, transcendentals=0
        ),
    )(*pieces, joined, swapped, *extra)


def factor_grads(far, joined, swapped, total, gram, targets, up):
    tokens, columns = targets.shape
    rank = up.shape[0]
    rows_out = rank // SEQ
    half = tokens // 2
    tn = (((0,), (0,)), ((), ()))

    def kernel(far0, far1, far2, far3, factor0, factor1, total_ref, gram_ref, t_ref, u_ref, out_ref, down_ref, upg_ref, sum_ref):
        tile = 512
        down_ref[...] = jnp.zeros((rank, columns), F32)
        upg_ref[...] = jnp.zeros((rank, columns), F32)
        sum_ref[...] = jnp.zeros((16, 128), F32)

        def half_of(base, far_refs):
            def rows_of(i, carry):
                inner = pl.ds(pl.multiple_of(i * tile, tile), tile)
                rows = pl.ds(pl.multiple_of(base + i * tile, tile), tile)
                products = total_ref[rows, : 2 * rank]
                squares = total_ref[rows, 2 * rank :]
                for ref, factor_ref in zip(far_refs, (factor0, factor1)):
                    block = ref[inner, :]
                    factor = factor_ref[2 * columns : 3 * columns, :]
                    products += jnp.dot(block, factor, preferred_element_type=F32)
                    wide = block.astype(F32)
                    for c in range(0, columns, 128):
                        squares += wide[:, c : c + 128] * wide[:, c : c + 128]
                latent = products[:, :rank].astype(BF16)
                across = products[:, rank:]
                grad = across
                for k in range(2):
                    grad -= jnp.dot(latent, gram_ref[k], preferred_element_type=F32)
                fit = latent.astype(F32) * (across + grad)
                energy = jnp.sum(squares, axis=1, keepdims=True)
                misfit = energy - jnp.sum(fit, axis=1, keepdims=True)
                own = t_ref[rows, :]
                rest = own.astype(F32) - jnp.dot(latent, u_ref[...], preferred_element_type=F32)
                high = rest.astype(BF16)
                low = (rest - high.astype(F32)).astype(BF16)
                upg_ref[...] += lax.dot_general(latent, high, tn, preferred_element_type=F32) + lax.dot_general(
                    latent, low, tn, preferred_element_type=F32
                )
                down_ref[...] += lax.dot_general(grad.astype(BF16), own, tn, preferred_element_type=F32)
                lane = lax.broadcasted_iota(jnp.int32, (1, 128), 1)
                sum_ref[0:1, :] += jnp.where(lane == 0, jnp.sum(energy), jnp.where(lane == 1, jnp.sum(misfit), 0.0))
                return carry

            lax.fori_loop(0, half // tile, rows_of, 0)

        half_of(0, (far0, far2))
        half_of(half, (far1, far3))
        lane = lax.broadcasted_iota(jnp.int32, (1, 128), 1)
        energy = jnp.sum(jnp.where(lane == 0, sum_ref[0:1, :], 0.0))
        misfit = jnp.sum(jnp.where(lane == 1, sum_ref[0:1, :], 0.0))
        tail = spread(lax.broadcasted_iota(jnp.int32, (rows_out, 128), 1), energy, misfit).astype(BF16)
        for s in range(SEQ):
            rows = slice(s * rows_out, (s + 1) * rows_out)
            out_ref[s, :, 0:columns] = down_ref[rows, :].astype(BF16)
            out_ref[s, :, columns : 2 * columns] = upg_ref[rows, :].astype(BF16)
            out_ref[s, :, 2 * columns :] = tail

    whole = pl.BlockSpec(memory_space=pltpu.VMEM)
    return pl.pallas_call(
        kernel,
        out_shape=jax.ShapeDtypeStruct((SEQ, rows_out, 2 * columns + 128), BF16),
        in_specs=[whole] * 10,
        out_specs=whole,
        scratch_shapes=[
            pltpu.VMEM((rank, columns), F32),
            pltpu.VMEM((rank, columns), F32),
            pltpu.VMEM((16, 128), F32),
        ],
        compiler_params=pltpu.CompilerParams(vmem_limit_bytes=24 * MIB),
    )(*far, joined, swapped, total, gram, targets, up)


def finish(parts, columns, tokens_all):
    blocks, rows, width = parts.shape
    entries = tokens_all * 2 * KEY_VALUE_HEADS * HEAD_SIZE

    def kernel(p_ref, down_ref, up_ref, rel_ref):
        total = jnp.zeros((rows, width), F32)
        for s in range(blocks):
            total += p_ref[s].astype(F32)
        tail = total[0:1, 2 * columns :]
        lane = lax.broadcasted_iota(jnp.int32, tail.shape, 1)
        energy = jnp.sum(jnp.where(lane < 3, tail, 0.0), keepdims=True)
        misfit = jnp.sum(jnp.where((lane >= 3) & (lane < 6), tail, 0.0), keepdims=True)
        factor = -(entries / energy) / math.sqrt(tokens_all)
        down_ref[...] = total[:, :columns] * factor
        up_ref[...] = total[:, columns : 2 * columns] * factor
        rel_ref[...] = misfit / energy

    whole = pl.BlockSpec(memory_space=pltpu.VMEM)
    return pl.pallas_call(
        kernel,
        out_shape=[
            jax.ShapeDtypeStruct((rows, columns), F32),
            jax.ShapeDtypeStruct((rows, columns), F32),
            jax.ShapeDtypeStruct((1, 1), F32),
        ],
        in_specs=[whole],
        out_specs=[whole] * 3,
        compiler_params=pltpu.CompilerParams(vmem_limit_bytes=4 * MIB),
    )(parts)


def per_device(hidden, key_value_weight, down_projection, up_projection, positions):
    rows_here = hidden.shape[0]
    tokens_all = lax.axis_size("seq") * rows_here
    swap = head_swap()
    half_dim = HEAD_SIZE // 2
    freqs = jnp.power(F32(THETA), -(jnp.arange(half_dim, dtype=F32) * 2.0 / HEAD_SIZE))
    angle = positions.astype(F32)[:, None] * freqs[None, :]
    cosine, sine = jnp.cos(angle), jnp.sin(angle)
    cosine = jnp.concatenate([cosine, cosine], axis=1)
    sine = jnp.concatenate([-sine, sine], axis=1)
    total, far_columns, last, factors, (cosine, sine) = gather(
        hidden, key_value_weight, down_projection, up_projection, (cosine, sine)
    )
    ordered = lax.optimization_barrier
    columns = factors[0].shape[0]
    total, *factors = ordered((total, *factors))
    joined = jnp.concatenate(factors, axis=0)
    targets = dense_last(far_columns, total, last, cosine, sine)
    targets, joined = ordered((targets, joined))
    half = rows_here // 2
    below = lax.ppermute(targets, "head", y_shift(1))
    above = lax.ppermute(targets, "head", y_shift(-1))
    partner = lax.ppermute(targets, "head", swap)
    swapped = lax.ppermute(joined, "head", swap)
    total = head_products([targets, partner], joined, swapped, (0,), None)
    below, above, total = ordered((below, above, total))
    far = [lax.ppermute(below[:half], "head", y_shift(1)), lax.ppermute(above[half:], "head", y_shift(-1))]
    pieces = [below, lax.ppermute(below, "head", swap), above, lax.ppermute(above, "head", swap)]
    total = head_products(pieces, joined, swapped, (1, 3), total)
    gram = gram_terms(joined, swapped)
    *far, total, gram = ordered((*far, total, gram))
    far += [lax.ppermute(rows, "head", swap) for rows in far]
    parts = factor_grads(far, joined, swapped, total, gram, targets, up_projection)
    parts = lax.all_to_all(parts, "seq", 0, 0)
    grad_down, grad_up, rel_error = finish(parts, HEAD_COLUMNS, tokens_all)
    return grad_down, grad_up, rel_error.reshape(())


def solution(mesh):
    return jax.shard_map(
        per_device,
        mesh=mesh,
        in_specs=(P("seq", None), P("seq", "head"), P("head", None), P(None, "head"), P("seq")),
        out_specs=(P("seq", "head"), P("seq", "head"), P()),
        check_vma=False,
    )
```

```python
import math

import jax
import jax.numpy as jnp
from jax import lax
from jax.experimental import pallas as pl
from jax.experimental.pallas import tpu as pltpu
from jax.sharding import PartitionSpec as P

KEY_VALUE_HEADS = 8
HEAD_SIZE = 128
HEAD_COLUMNS = 2 * HEAD_SIZE
LATENT_RANK = 512
THETA = 500000.0
X, Y, Z, HEADS = 4, 4, 8, 8
SEQ = X * Z
MIB = 1024 * 1024
F32 = jnp.float32
BF16 = jnp.bfloat16


def z_shift(k):
    return [(x * Z + z, x * Z + (z + k) % Z) for x in range(X) for z in range(Z)]


def x_shift(k):
    return [(x * Z + z, ((x + k) % X) * Z + z) for x in range(X) for z in range(Z)]


def y_shift(k):
    return [(y * 2 + c, ((y + k) % Y) * 2 + c) for y in range(Y) for c in range(2)]


def head_swap():
    return [(h, h ^ 1) for h in range(HEADS)]


def both_ways(up, down, axis, shift):
    return lax.ppermute(up, axis, shift(1)), lax.ppermute(down, axis, shift(-1))


def halves(up, down, axis, shift):
    half = up.shape[0] // 2
    return both_ways(up[:half], down[half:], axis, shift)


def gather(hidden, weight, down, up, turn):
    ordered = lax.optimization_barrier
    part_rows = weight.shape[0] // 2
    part_a, part_b = weight[:part_rows], weight[part_rows:]
    b_order, a_order = [0, -1, 1, 2], [0, -1, 1, -2, 2, -3, 3, 4]

    def column(dx):
        return [(dx, dz, 0) for dz in a_order]

    def row(dz):
        return [(dx, dz, 1) for dx in b_order]

    b_near = both_ways(part_b, part_b, "seq", x_shift)
    b_far = lax.ppermute(part_b, "seq", x_shift(X // 2))
    a_first = both_ways(part_a, part_a, "seq", z_shift)
    b_all = jnp.concatenate([part_b, *b_near, b_far], axis=0)
    down, up, *a_first = ordered((down, up, *a_first))
    factors = [head_factors(down, up)]
    for _ in range(Y - 1):
        factors.append(lax.ppermute(factors[-1], "head", y_shift(1)))
    b_first = both_ways(b_all, b_all, "seq", z_shift)
    a_second = both_ways(*a_first, "seq", z_shift)
    a_third = both_ways(*a_second, "seq", z_shift)
    pieces = [(b_all, row(0)), (b_first[0], row(-1)), (b_first[1], row(1))]
    (total,) = dense_step(hidden, pieces, None, [])
    *a_third, total = ordered((*a_third, total))
    b_second = both_ways(*b_first, "seq", z_shift)
    a_end = halves(*a_third, "seq", z_shift)
    a_all = jnp.concatenate([part_a, *a_first, *a_second, *a_third, *a_end], axis=0)
    a_x = both_ways(a_all, a_all, "seq", x_shift)
    b_third = both_ways(*b_second, "seq", z_shift)
    (total,) = dense_step(hidden, [(a_all, column(0)), (b_second[0], row(-2)), (b_second[1], row(2))], total, [])
    *a_x, total, cosine, sine = ordered((*a_x, total, *turn))
    a_last = halves(*a_x, "seq", x_shift)
    b_last = halves(*b_third, "seq", z_shift)
    last = [(a_last[0], column(X // 2)[: Z // 2]), (a_last[1], column(X // 2)[Z // 2 :])]
    last += [(b_last[0], row(Z // 2)[: X // 2]), (b_last[1], row(Z // 2)[X // 2 :])]
    missing = [entry for _, entries in last for entry in entries]
    pieces = [(a_x[0], column(-1)), (a_x[1], column(1)), (b_third[0], row(-3)), (b_third[1], row(3))]
    total, far_columns = dense_step(hidden, pieces, total, missing)
    return total, far_columns, last, factors, (cosine, sine)


def column_of(entry):
    dx, dz, part = entry
    here = lax.axis_index("seq")
    owner = ((here // Z + dx + X) % X) * Z + (here % Z + dz + Z) % Z
    return pl.multiple_of(owner * 256 + part * 128, 128)


def dense_step(hidden, pieces, total, missing):
    rows = hidden.shape[0]
    columns = pieces[0][0].shape[1]
    entries = [entry for _, group in pieces for entry in group]
    count, extra = len(pieces), [] if total is None else [total]

    def kernel(hidden_ref, *refs):
        piece_refs, extra_refs = refs[:count], refs[count : count + len(extra)]
        out_refs, (block_ref, sems) = refs[count + len(extra) : -2], refs[-2:]
        out_ref = out_refs[0]

        def columns_to(entry, to_ref, i, sem):
            return pltpu.make_async_copy(
                hidden_ref.at[:, pl.ds(column_of(entry), 128)], to_ref.at[:, i * 128 : (i + 1) * 128], sems.at[sem]
            )

        copies = [columns_to(entry, block_ref, i, i) for i, entry in enumerate(entries)]
        copies += [columns_to(entry, out_refs[1], i, len(entries) + i) for i, entry in enumerate(missing)]
        for copy in copies:
            copy.start()
        start = 0
        for k, ref in enumerate(piece_refs):
            depth = ref.shape[0]
            for copy in copies[start // 128 : (start + depth) // 128]:
                copy.wait()
            product = jnp.dot(block_ref[:, start : start + depth], ref[...], preferred_element_type=F32)
            if k > 0:
                out_ref[...] += product
            else:
                out_ref[...] = extra_refs[0][...] + product if extra else product
            start += depth
        for copy in copies[len(entries) :]:
            copy.wait()

    whole = pl.BlockSpec(memory_space=pltpu.VMEM)
    out_shape = [jax.ShapeDtypeStruct((rows, columns), F32)]
    if missing:
        out_shape.append(jax.ShapeDtypeStruct((rows, 128 * len(missing)), BF16))
    return pl.pallas_call(
        kernel,
        out_shape=out_shape,
        in_specs=[pl.BlockSpec(memory_space=pltpu.HBM)] + [whole] * (count + len(extra)),
        out_specs=[whole] * len(out_shape),
        scratch_shapes=[
            pltpu.VMEM((rows, 128 * len(entries)), BF16),
            pltpu.SemaphoreType.DMA((len(entries) + len(missing),)),
        ],
        compiler_params=pltpu.CompilerParams(vmem_limit_bytes=44 * MIB),
        cost_estimate=pl.CostEstimate(
            flops=256 * rows * len(entries) * columns, bytes_accessed=256 * rows * len(entries), transcendentals=0
        ),
    )(hidden, *[rows_ for rows_, _ in pieces], *extra)


def dense_last(far, total, last, cosine, sine):
    rows, columns = total.shape

    def kernel(far_ref, total_ref, cos_ref, sin_ref, *rest):
        piece_refs, out_ref = rest[:-1], rest[-1]
        tile = 256
        for row in range(0, rows, tile):
            here = slice(row, row + tile)
            dense = total_ref[here, :]
            start = 0
            for ref in piece_refs:
                depth = ref.shape[0]
                dense += jnp.dot(far_ref[here, start : start + depth], ref[...], preferred_element_type=F32)
                start += depth
            keys = dense[:, :HEAD_SIZE]
            turned = keys * cos_ref[here, :] + pltpu.roll(keys, HEAD_SIZE // 2, 1) * sin_ref[here, :]
            out_ref[here, :HEAD_SIZE] = turned.astype(BF16)
            out_ref[here, HEAD_SIZE:] = dense[:, HEAD_SIZE:].astype(BF16)

    whole = pl.BlockSpec(memory_space=pltpu.VMEM)
    return pl.pallas_call(
        kernel,
        out_shape=jax.ShapeDtypeStruct((rows, columns), BF16),
        in_specs=[whole] * (4 + len(last)),
        out_specs=whole,
        compiler_params=pltpu.CompilerParams(vmem_limit_bytes=16 * MIB),
    )(far, total, cosine, sine, *[rows_ for rows_, _ in last])


def split3(value):
    high = value.astype(BF16).astype(F32)
    middle = (value - high).astype(BF16).astype(F32)
    return high, middle, value - high - middle


def spread(lane, first, second):
    out = jnp.zeros(lane.shape, F32)
    for i, part in enumerate((*split3(first), *split3(second))):
        out = jnp.where(lane == i, part, out)
    return out


def head_factors(down, up):
    columns, rank = down.shape

    def kernel(d_ref, u_ref, out_ref):
        out_ref[:, :rank] = d_ref[...]
        out_ref[:, rank:] = u_ref[...].astype(F32).T.astype(BF16)

    whole = pl.BlockSpec(memory_space=pltpu.VMEM)
    return pl.pallas_call(
        kernel,
        out_shape=jax.ShapeDtypeStruct((columns, 2 * rank), BF16),
        in_specs=[whole] * 2,
        out_specs=whole,
        compiler_params=pltpu.CompilerParams(vmem_limit_bytes=4 * MIB),
    )(down, up)


def gram_terms(joined, swapped):
    rank = joined.shape[1] // 2

    def kernel(joined_ref, swapped_ref, out_ref):
        gram = jnp.zeros((rank, rank), F32)
        for ref in (joined_ref, swapped_ref):
            part = ref[:, rank:]
            gram += lax.dot_general(part, part, (((0,), (0,)), ((), ())), preferred_element_type=F32)
        high = gram.astype(BF16)
        out_ref[0] = high
        out_ref[1] = (gram - high.astype(F32)).astype(BF16)

    whole = pl.BlockSpec(memory_space=pltpu.VMEM)
    return pl.pallas_call(
        kernel,
        out_shape=jax.ShapeDtypeStruct((2, rank, rank), BF16),
        in_specs=[whole] * 2,
        out_specs=whole,
        compiler_params=pltpu.CompilerParams(vmem_limit_bytes=16 * MIB),
    )(joined, swapped)


def head_products(pieces, joined, swapped, chips, total):
    tokens, columns = pieces[0].shape
    rank = joined.shape[1] // 2
    count = len(pieces)
    extra = [] if total is None else [total]

    def kernel(*refs):
        piece_refs, factor_refs, extra_refs, out_ref = refs[:count], refs[count : count + 2], refs[count + 2 : -1], refs[-1]
        tile = 256

        def rows_of(i, carry):
            rows = pl.ds(pl.multiple_of(i * tile, tile), tile)
            products = extra_refs[0][rows, : 2 * rank] if extra else jnp.zeros((tile, 2 * rank), F32)
            squares = extra_refs[0][rows, 2 * rank :] if extra else jnp.zeros((tile, 128), F32)
            for k, ref in enumerate(piece_refs):
                block = ref[rows, :]
                chip = chips[k // 2]
                factor = factor_refs[k % 2][chip * columns : (chip + 1) * columns, :]
                products += jnp.dot(block, factor, preferred_element_type=F32)
                wide = block.astype(F32)
                for c in range(0, columns, 128):
                    squares += wide[:, c : c + 128] * wide[:, c : c + 128]
            out_ref[rows, : 2 * rank] = products
            out_ref[rows, 2 * rank :] = squares
            return carry

        lax.fori_loop(0, tokens // tile, rows_of, 0)

    whole = pl.BlockSpec(memory_space=pltpu.VMEM)
    return pl.pallas_call(
        kernel,
        out_shape=jax.ShapeDtypeStruct((tokens, 2 * rank + 128), F32),
        in_specs=[whole] * (count + 2 + len(extra)),
        out_specs=whole,
        compiler_params=pltpu.CompilerParams(vmem_limit_bytes=24 * MIB),
        cost_estimate=pl.CostEstimate(
            flops=4 * tokens * columns * rank * count, bytes_accessed=2 * tokens * columns, transcendentals=0
        ),
    )(*pieces, joined, swapped, *extra)


def factor_grads(far, joined, swapped, total, gram, targets, up):
    tokens, columns = targets.shape
    rank = up.shape[0]
    rows_out = rank // SEQ
    half = tokens // 2
    tn = (((0,), (0,)), ((), ()))

    def kernel(far0, far1, far2, far3, factor0, factor1, total_ref, gram_ref, t_ref, u_ref, out_ref, down_ref, upg_ref, sum_ref):
        tile = 512
        down_ref[...] = jnp.zeros((rank, columns), F32)
        upg_ref[...] = jnp.zeros((rank, columns), F32)
        sum_ref[...] = jnp.zeros((16, 128), F32)

        def half_of(base, far_refs):
            def rows_of(i, carry):
                inner = pl.ds(pl.multiple_of(i * tile, tile), tile)
                rows = pl.ds(pl.multiple_of(base + i * tile, tile), tile)
                products = total_ref[rows, : 2 * rank]
                squares = total_ref[rows, 2 * rank :]
                for ref, factor_ref in zip(far_refs, (factor0, factor1)):
                    block = ref[inner, :]
                    factor = factor_ref[2 * columns : 3 * columns, :]
                    products += jnp.dot(block, factor, preferred_element_type=F32)
                    wide = block.astype(F32)
                    for c in range(0, columns, 128):
                        squares += wide[:, c : c + 128] * wide[:, c : c + 128]
                latent = products[:, :rank].astype(BF16)
                across = products[:, rank:]
                grad = across
                for k in range(2):
                    grad -= jnp.dot(latent, gram_ref[k], preferred_element_type=F32)
                fit = latent.astype(F32) * (across + grad)
                energy = jnp.sum(squares, axis=1, keepdims=True)
                misfit = energy - jnp.sum(fit, axis=1, keepdims=True)
                own = t_ref[rows, :]
                rest = own.astype(F32) - jnp.dot(latent, u_ref[...], preferred_element_type=F32)
                high = rest.astype(BF16)
                low = (rest - high.astype(F32)).astype(BF16)
                upg_ref[...] += lax.dot_general(latent, high, tn, preferred_element_type=F32) + lax.dot_general(
                    latent, low, tn, preferred_element_type=F32
                )
                down_ref[...] += lax.dot_general(grad.astype(BF16), own, tn, preferred_element_type=F32)
                lane = lax.broadcasted_iota(jnp.int32, (1, 128), 1)
                sum_ref[0:1, :] += jnp.where(lane == 0, jnp.sum(energy), jnp.where(lane == 1, jnp.sum(misfit), 0.0))
                return carry

            lax.fori_loop(0, half // tile, rows_of, 0)

        half_of(0, (far0, far2))
        half_of(half, (far1, far3))
        lane = lax.broadcasted_iota(jnp.int32, (1, 128), 1)
        energy = jnp.sum(jnp.where(lane == 0, sum_ref[0:1, :], 0.0))
        misfit = jnp.sum(jnp.where(lane == 1, sum_ref[0:1, :], 0.0))
        tail = spread(lax.broadcasted_iota(jnp.int32, (rows_out, 128), 1), energy, misfit).astype(BF16)
        for s in range(SEQ):
            rows = slice(s * rows_out, (s + 1) * rows_out)
            out_ref[s, :, 0:columns] = down_ref[rows, :].astype(BF16)
            out_ref[s, :, columns : 2 * columns] = upg_ref[rows, :].astype(BF16)
            out_ref[s, :, 2 * columns :] = tail

    whole = pl.BlockSpec(memory_space=pltpu.VMEM)
    return pl.pallas_call(
        kernel,
        out_shape=jax.ShapeDtypeStruct((SEQ, rows_out, 2 * columns + 128), BF16),
        in_specs=[whole] * 10,
        out_specs=whole,
        scratch_shapes=[
            pltpu.VMEM((rank, columns), F32),
            pltpu.VMEM((rank, columns), F32),
            pltpu.VMEM((16, 128), F32),
        ],
        compiler_params=pltpu.CompilerParams(vmem_limit_bytes=24 * MIB),
    )(*far, joined, swapped, total, gram, targets, up)


def finish(parts, columns, tokens_all):
    blocks, rows, width = parts.shape
    entries = tokens_all * 2 * KEY_VALUE_HEADS * HEAD_SIZE

    def kernel(p_ref, down_ref, up_ref, rel_ref):
        total = jnp.zeros((rows, width), F32)
        for s in range(blocks):
            total += p_ref[s].astype(F32)
        tail = total[0:1, 2 * columns :]
        lane = lax.broadcasted_iota(jnp.int32, tail.shape, 1)
        energy = jnp.sum(jnp.where(lane < 3, tail, 0.0), keepdims=True)
        misfit = jnp.sum(jnp.where((lane >= 3) & (lane < 6), tail, 0.0), keepdims=True)
        factor = -(entries / energy) / math.sqrt(tokens_all)
        down_ref[...] = total[:, :columns] * factor
        up_ref[...] = total[:, columns : 2 * columns] * factor
        rel_ref[...] = misfit / energy

    whole = pl.BlockSpec(memory_space=pltpu.VMEM)
    return pl.pallas_call(
        kernel,
        out_shape=[
            jax.ShapeDtypeStruct((rows, columns), F32),
            jax.ShapeDtypeStruct((rows, columns), F32),
            jax.ShapeDtypeStruct((1, 1), F32),
        ],
        in_specs=[whole],
        out_specs=[whole] * 3,
        compiler_params=pltpu.CompilerParams(vmem_limit_bytes=4 * MIB),
    )(parts)


def per_device(hidden, key_value_weight, down_projection, up_projection, positions):
    rows_here = hidden.shape[0]
    tokens_all = lax.axis_size("seq") * rows_here
    swap = head_swap()
    half_dim = HEAD_SIZE // 2
    freqs = jnp.power(F32(THETA), -(jnp.arange(half_dim, dtype=F32) * 2.0 / HEAD_SIZE))
    angle = positions.astype(F32)[:, None] * freqs[None, :]
    cosine, sine = jnp.cos(angle), jnp.sin(angle)
    cosine = jnp.concatenate([cosine, cosine], axis=1)
    sine = jnp.concatenate([-sine, sine], axis=1)
    total, far_columns, last, factors, (cosine, sine) = gather(
        hidden, key_value_weight, down_projection, up_projection, (cosine, sine)
    )
    ordered = lax.optimization_barrier
    columns = factors[0].shape[0]
    total, *factors = ordered((total, *factors))
    joined = jnp.concatenate(factors, axis=0)
    targets = dense_last(far_columns, total, last, cosine, sine)
    targets, joined = ordered((targets, joined))
    half = rows_here // 2
    below = lax.ppermute(targets, "head", y_shift(1))
    above = lax.ppermute(targets, "head", y_shift(-1))
    partner = lax.ppermute(targets, "head", swap)
    swapped = lax.ppermute(joined, "head", swap)
    total = head_products([targets, partner], joined, swapped, (0,), None)
    below, above, total = ordered((below, above, total))
    far = [lax.ppermute(below[:half], "head", y_shift(1)), lax.ppermute(above[half:], "head", y_shift(-1))]
    pieces = [below, lax.ppermute(below, "head", swap), above, lax.ppermute(above, "head", swap)]
    total = head_products(pieces, joined, swapped, (1, 3), total)
    gram = gram_terms(joined, swapped)
    *far, total, gram = ordered((*far, total, gram))
    far += [lax.ppermute(rows, "head", swap) for rows in far]
    parts = factor_grads(far, joined, swapped, total, gram, targets, up_projection)
    parts = lax.all_to_all(parts, "seq", 0, 0)
    grad_down, grad_up, rel_error = finish(parts, HEAD_COLUMNS, tokens_all)
    return grad_down, grad_up, rel_error.reshape(())


def solution(mesh):
    return jax.shard_map(
        per_device,
        mesh=mesh,
        in_specs=(P("seq", None), P("seq", "head"), P("head", None), P(None, "head"), P("seq")),
        out_specs=(P("seq", "head"), P("seq", "head"), P()),
        check_vma=False,
    )
```

```python
import math

import jax
import jax.numpy as jnp
from jax import lax
from jax.experimental import pallas as pl
from jax.experimental.pallas import tpu as pltpu
from jax.sharding import PartitionSpec as P

KEY_VALUE_HEADS = 8
HEAD_SIZE = 128
HEAD_COLUMNS = 2 * HEAD_SIZE
LATENT_RANK = 512
THETA = 500000.0
X, Y, Z, HEADS = 4, 4, 8, 8
SEQ = X * Z
MIB = 1024 * 1024
F32 = jnp.float32
BF16 = jnp.bfloat16


def z_shift(k):
    return [(x * Z + z, x * Z + (z + k) % Z) for x in range(X) for z in range(Z)]


def x_shift(k):
    return [(x * Z + z, ((x + k) % X) * Z + z) for x in range(X) for z in range(Z)]


def y_shift(k):
    return [(y * 2 + c, ((y + k) % Y) * 2 + c) for y in range(Y) for c in range(2)]


def head_swap():
    return [(h, h ^ 1) for h in range(HEADS)]


def both_ways(up, down, axis, shift):
    return lax.ppermute(up, axis, shift(1)), lax.ppermute(down, axis, shift(-1))


def halves(up, down, axis, shift):
    half = up.shape[0] // 2
    return both_ways(up[:half], down[half:], axis, shift)


def gather(hidden, weight, down, up, turn):
    ordered = lax.optimization_barrier
    own = head_factors(down, up)
    weight, own = ordered((weight, own))
    part_rows = weight.shape[0] // 2
    part_a, part_b = weight[:part_rows], weight[part_rows:]
    b_order, a_order = [0, -1, 1, 2], [0, -1, 1, -2, 2, -3, 3, 4]

    def column(dx):
        return [(dx, dz, 0) for dz in a_order]

    def row(dz):
        return [(dx, dz, 1) for dx in b_order]

    b_near = both_ways(part_b, part_b, "seq", x_shift)
    b_far = lax.ppermute(part_b, "seq", x_shift(X // 2))
    a_first = both_ways(part_a, part_a, "seq", z_shift)
    b_all = jnp.concatenate([part_b, *b_near, b_far], axis=0)
    factors = [own]
    for _ in range(Y - 1):
        factors.append(lax.ppermute(factors[-1], "head", y_shift(1)))
    b_first = both_ways(b_all, b_all, "seq", z_shift)
    a_second = both_ways(*a_first, "seq", z_shift)
    a_third = both_ways(*a_second, "seq", z_shift)
    pieces = [(b_all, row(0)), (b_first[0], row(-1)), (b_first[1], row(1))]
    (total,) = dense_step(hidden, pieces, None, [])
    *a_third, total = ordered((*a_third, total))
    b_second = both_ways(*b_first, "seq", z_shift)
    a_end = halves(*a_third, "seq", z_shift)
    a_all = jnp.concatenate([part_a, *a_first, *a_second, *a_third, *a_end], axis=0)
    a_x = both_ways(a_all, a_all, "seq", x_shift)
    b_third = both_ways(*b_second, "seq", z_shift)
    (total,) = dense_step(hidden, [(a_all, column(0)), (b_second[0], row(-2)), (b_second[1], row(2))], total, [])
    *a_x, total, cosine, sine = ordered((*a_x, total, *turn))
    a_last = halves(*a_x, "seq", x_shift)
    b_last = halves(*b_third, "seq", z_shift)
    last = [(a_last[0], column(X // 2)[: Z // 2]), (a_last[1], column(X // 2)[Z // 2 :])]
    last += [(b_last[0], row(Z // 2)[: X // 2]), (b_last[1], row(Z // 2)[X // 2 :])]
    missing = [entry for _, entries in last for entry in entries]
    pieces = [(a_x[0], column(-1)), (a_x[1], column(1)), (b_third[0], row(-3)), (b_third[1], row(3))]
    total, far_columns = dense_step(hidden, pieces, total, missing)
    return total, far_columns, last, factors, (cosine, sine)


def column_of(entry):
    dx, dz, part = entry
    here = lax.axis_index("seq")
    owner = ((here // Z + dx + X) % X) * Z + (here % Z + dz + Z) % Z
    return pl.multiple_of(owner * 256 + part * 128, 128)


def dense_step(hidden, pieces, total, missing):
    rows = hidden.shape[0]
    columns = pieces[0][0].shape[1]
    entries = [entry for _, group in pieces for entry in group]
    count, extra = len(pieces), [] if total is None else [total]

    def kernel(hidden_ref, *refs):
        piece_refs, extra_refs = refs[:count], refs[count : count + len(extra)]
        out_refs, (block_ref, sems) = refs[count + len(extra) : -2], refs[-2:]
        out_ref = out_refs[0]

        def columns_to(entry, to_ref, i, sem):
            return pltpu.make_async_copy(
                hidden_ref.at[:, pl.ds(column_of(entry), 128)], to_ref.at[:, i * 128 : (i + 1) * 128], sems.at[sem]
            )

        copies = [columns_to(entry, block_ref, i, i) for i, entry in enumerate(entries)]
        copies += [columns_to(entry, out_refs[1], i, len(entries) + i) for i, entry in enumerate(missing)]
        for copy in copies:
            copy.start()
        start = 0
        for k, ref in enumerate(piece_refs):
            depth = ref.shape[0]
            for copy in copies[start // 128 : (start + depth) // 128]:
                copy.wait()
            product = jnp.dot(block_ref[:, start : start + depth], ref[...], preferred_element_type=F32)
            if k > 0:
                out_ref[...] += product
            else:
                out_ref[...] = extra_refs[0][...] + product if extra else product
            start += depth
        for copy in copies[len(entries) :]:
            copy.wait()

    whole = pl.BlockSpec(memory_space=pltpu.VMEM)
    out_shape = [jax.ShapeDtypeStruct((rows, columns), F32)]
    if missing:
        out_shape.append(jax.ShapeDtypeStruct((rows, 128 * len(missing)), BF16))
    return pl.pallas_call(
        kernel,
        out_shape=out_shape,
        in_specs=[pl.BlockSpec(memory_space=pltpu.HBM)] + [whole] * (count + len(extra)),
        out_specs=[whole] * len(out_shape),
        scratch_shapes=[
            pltpu.VMEM((rows, 128 * len(entries)), BF16),
            pltpu.SemaphoreType.DMA((len(entries) + len(missing),)),
        ],
        compiler_params=pltpu.CompilerParams(vmem_limit_bytes=44 * MIB),
        cost_estimate=pl.CostEstimate(
            flops=256 * rows * len(entries) * columns, bytes_accessed=256 * rows * len(entries), transcendentals=0
        ),
    )(hidden, *[rows_ for rows_, _ in pieces], *extra)


def dense_last(far, total, last, cosine, sine):
    rows, columns = total.shape

    def kernel(far_ref, total_ref, cos_ref, sin_ref, *rest):
        piece_refs, out_ref = rest[:-1], rest[-1]
        tile = 256
        for row in range(0, rows, tile):
            here = slice(row, row + tile)
            dense = total_ref[here, :]
            start = 0
            for ref in piece_refs:
                depth = ref.shape[0]
                dense += jnp.dot(far_ref[here, start : start + depth], ref[...], preferred_element_type=F32)
                start += depth
            keys = dense[:, :HEAD_SIZE]
            turned = keys * cos_ref[here, :] + pltpu.roll(keys, HEAD_SIZE // 2, 1) * sin_ref[here, :]
            out_ref[here, :HEAD_SIZE] = turned.astype(BF16)
            out_ref[here, HEAD_SIZE:] = dense[:, HEAD_SIZE:].astype(BF16)

    whole = pl.BlockSpec(memory_space=pltpu.VMEM)
    return pl.pallas_call(
        kernel,
        out_shape=jax.ShapeDtypeStruct((rows, columns), BF16),
        in_specs=[whole] * (4 + len(last)),
        out_specs=whole,
        compiler_params=pltpu.CompilerParams(vmem_limit_bytes=16 * MIB),
    )(far, total, cosine, sine, *[rows_ for rows_, _ in last])


def split3(value):
    high = value.astype(BF16).astype(F32)
    middle = (value - high).astype(BF16).astype(F32)
    return high, middle, value - high - middle


def spread(lane, first, second):
    out = jnp.zeros(lane.shape, F32)
    for i, part in enumerate((*split3(first), *split3(second))):
        out = jnp.where(lane == i, part, out)
    return out


def head_factors(down, up):
    columns, rank = down.shape

    def kernel(d_ref, u_ref, out_ref):
        out_ref[:, :rank] = d_ref[...]
        out_ref[:, rank:] = u_ref[...].astype(F32).T.astype(BF16)

    whole = pl.BlockSpec(memory_space=pltpu.VMEM)
    return pl.pallas_call(
        kernel,
        out_shape=jax.ShapeDtypeStruct((columns, 2 * rank), BF16),
        in_specs=[whole] * 2,
        out_specs=whole,
        compiler_params=pltpu.CompilerParams(vmem_limit_bytes=4 * MIB),
    )(down, up)


def gram_terms(joined, swapped):
    rank = joined.shape[1] // 2

    def kernel(joined_ref, swapped_ref, out_ref):
        gram = jnp.zeros((rank, rank), F32)
        for ref in (joined_ref, swapped_ref):
            part = ref[:, rank:]
            gram += lax.dot_general(part, part, (((0,), (0,)), ((), ())), preferred_element_type=F32)
        high = gram.astype(BF16)
        out_ref[0] = high
        out_ref[1] = (gram - high.astype(F32)).astype(BF16)

    whole = pl.BlockSpec(memory_space=pltpu.VMEM)
    return pl.pallas_call(
        kernel,
        out_shape=jax.ShapeDtypeStruct((2, rank, rank), BF16),
        in_specs=[whole] * 2,
        out_specs=whole,
        compiler_params=pltpu.CompilerParams(vmem_limit_bytes=16 * MIB),
    )(joined, swapped)


def head_products(pieces, joined, swapped, chips, total):
    tokens, columns = pieces[0].shape
    rank = joined.shape[1] // 2
    count = len(pieces)
    extra = [] if total is None else [total]

    def kernel(*refs):
        piece_refs, factor_refs, extra_refs, out_ref = refs[:count], refs[count : count + 2], refs[count + 2 : -1], refs[-1]
        tile = 256

        def rows_of(i, carry):
            rows = pl.ds(pl.multiple_of(i * tile, tile), tile)
            products = extra_refs[0][rows, : 2 * rank] if extra else jnp.zeros((tile, 2 * rank), F32)
            squares = extra_refs[0][rows, 2 * rank :] if extra else jnp.zeros((tile, 128), F32)
            for k, ref in enumerate(piece_refs):
                block = ref[rows, :]
                chip = chips[k // 2]
                factor = factor_refs[k % 2][chip * columns : (chip + 1) * columns, :]
                products += jnp.dot(block, factor, preferred_element_type=F32)
                wide = block.astype(F32)
                for c in range(0, columns, 128):
                    squares += wide[:, c : c + 128] * wide[:, c : c + 128]
            out_ref[rows, : 2 * rank] = products
            out_ref[rows, 2 * rank :] = squares
            return carry

        lax.fori_loop(0, tokens // tile, rows_of, 0)

    whole = pl.BlockSpec(memory_space=pltpu.VMEM)
    return pl.pallas_call(
        kernel,
        out_shape=jax.ShapeDtypeStruct((tokens, 2 * rank + 128), F32),
        in_specs=[whole] * (count + 2 + len(extra)),
        out_specs=whole,
        compiler_params=pltpu.CompilerParams(vmem_limit_bytes=24 * MIB),
        cost_estimate=pl.CostEstimate(
            flops=4 * tokens * columns * rank * count, bytes_accessed=2 * tokens * columns, transcendentals=0
        ),
    )(*pieces, joined, swapped, *extra)


def factor_grads(far, joined, swapped, total, gram, targets, up):
    tokens, columns = targets.shape
    rank = up.shape[0]
    rows_out = rank // SEQ
    half = tokens // 2
    tn = (((0,), (0,)), ((), ()))

    def kernel(far0, far1, far2, far3, factor0, factor1, total_ref, gram_ref, t_ref, u_ref, out_ref, down_ref, upg_ref, sum_ref):
        tile = 512
        down_ref[...] = jnp.zeros((rank, columns), F32)
        upg_ref[...] = jnp.zeros((rank, columns), F32)
        sum_ref[...] = jnp.zeros((16, 128), F32)

        def half_of(base, far_refs):
            def rows_of(i, carry):
                inner = pl.ds(pl.multiple_of(i * tile, tile), tile)
                rows = pl.ds(pl.multiple_of(base + i * tile, tile), tile)
                products = total_ref[rows, : 2 * rank]
                squares = total_ref[rows, 2 * rank :]
                for ref, factor_ref in zip(far_refs, (factor0, factor1)):
                    block = ref[inner, :]
                    factor = factor_ref[2 * columns : 3 * columns, :]
                    products += jnp.dot(block, factor, preferred_element_type=F32)
                    wide = block.astype(F32)
                    for c in range(0, columns, 128):
                        squares += wide[:, c : c + 128] * wide[:, c : c + 128]
                latent = products[:, :rank].astype(BF16)
                across = products[:, rank:]
                grad = across
                for k in range(2):
                    grad -= jnp.dot(latent, gram_ref[k], preferred_element_type=F32)
                fit = latent.astype(F32) * (across + grad)
                energy = jnp.sum(squares, axis=1, keepdims=True)
                misfit = energy - jnp.sum(fit, axis=1, keepdims=True)
                own = t_ref[rows, :]
                rest = own.astype(F32) - jnp.dot(latent, u_ref[...], preferred_element_type=F32)
                high = rest.astype(BF16)
                low = (rest - high.astype(F32)).astype(BF16)
                upg_ref[...] += lax.dot_general(latent, high, tn, preferred_element_type=F32) + lax.dot_general(
                    latent, low, tn, preferred_element_type=F32
                )
                down_ref[...] += lax.dot_general(grad.astype(BF16), own, tn, preferred_element_type=F32)
                lane = lax.broadcasted_iota(jnp.int32, (1, 128), 1)
                sum_ref[0:1, :] += jnp.where(lane == 0, jnp.sum(energy), jnp.where(lane == 1, jnp.sum(misfit), 0.0))
                return carry

            lax.fori_loop(0, half // tile, rows_of, 0)

        half_of(0, (far0, far2))
        half_of(half, (far1, far3))
        lane = lax.broadcasted_iota(jnp.int32, (1, 128), 1)
        energy = jnp.sum(jnp.where(lane == 0, sum_ref[0:1, :], 0.0))
        misfit = jnp.sum(jnp.where(lane == 1, sum_ref[0:1, :], 0.0))
        tail = spread(lax.broadcasted_iota(jnp.int32, (rows_out, 128), 1), energy, misfit).astype(BF16)
        for s in range(SEQ):
            rows = slice(s * rows_out, (s + 1) * rows_out)
            out_ref[s, :, 0:columns] = down_ref[rows, :].astype(BF16)
            out_ref[s, :, columns : 2 * columns] = upg_ref[rows, :].astype(BF16)
            out_ref[s, :, 2 * columns :] = tail

    whole = pl.BlockSpec(memory_space=pltpu.VMEM)
    return pl.pallas_call(
        kernel,
        out_shape=jax.ShapeDtypeStruct((SEQ, rows_out, 2 * columns + 128), BF16),
        in_specs=[whole] * 10,
        out_specs=whole,
        scratch_shapes=[
            pltpu.VMEM((rank, columns), F32),
            pltpu.VMEM((rank, columns), F32),
            pltpu.VMEM((16, 128), F32),
        ],
        compiler_params=pltpu.CompilerParams(vmem_limit_bytes=24 * MIB),
    )(*far, joined, swapped, total, gram, targets, up)


def finish(parts, columns, tokens_all):
    blocks, rows, width = parts.shape
    entries = tokens_all * 2 * KEY_VALUE_HEADS * HEAD_SIZE

    def kernel(p_ref, down_ref, up_ref, rel_ref):
        total = jnp.zeros((rows, width), F32)
        for s in range(blocks):
            total += p_ref[s].astype(F32)
        tail = total[0:1, 2 * columns :]
        lane = lax.broadcasted_iota(jnp.int32, tail.shape, 1)
        energy = jnp.sum(jnp.where(lane < 3, tail, 0.0), keepdims=True)
        misfit = jnp.sum(jnp.where((lane >= 3) & (lane < 6), tail, 0.0), keepdims=True)
        factor = -(entries / energy) / math.sqrt(tokens_all)
        down_ref[...] = total[:, :columns] * factor
        up_ref[...] = total[:, columns : 2 * columns] * factor
        rel_ref[...] = misfit / energy

    whole = pl.BlockSpec(memory_space=pltpu.VMEM)
    return pl.pallas_call(
        kernel,
        out_shape=[
            jax.ShapeDtypeStruct((rows, columns), F32),
            jax.ShapeDtypeStruct((rows, columns), F32),
            jax.ShapeDtypeStruct((1, 1), F32),
        ],
        in_specs=[whole],
        out_specs=[whole] * 3,
        compiler_params=pltpu.CompilerParams(vmem_limit_bytes=4 * MIB),
    )(parts)


def per_device(hidden, key_value_weight, down_projection, up_projection, positions):
    rows_here = hidden.shape[0]
    tokens_all = lax.axis_size("seq") * rows_here
    swap = head_swap()
    half_dim = HEAD_SIZE // 2
    freqs = jnp.power(F32(THETA), -(jnp.arange(half_dim, dtype=F32) * 2.0 / HEAD_SIZE))
    angle = positions.astype(F32)[:, None] * freqs[None, :]
    cosine, sine = jnp.cos(angle), jnp.sin(angle)
    cosine = jnp.concatenate([cosine, cosine], axis=1)
    sine = jnp.concatenate([-sine, sine], axis=1)
    total, far_columns, last, factors, (cosine, sine) = gather(
        hidden, key_value_weight, down_projection, up_projection, (cosine, sine)
    )
    ordered = lax.optimization_barrier
    columns = factors[0].shape[0]
    total, *factors = ordered((total, *factors))
    joined = jnp.concatenate(factors, axis=0)
    targets = dense_last(far_columns, total, last, cosine, sine)
    targets, joined = ordered((targets, joined))
    half = rows_here // 2
    below = lax.ppermute(targets, "head", y_shift(1))
    above = lax.ppermute(targets, "head", y_shift(-1))
    partner = lax.ppermute(targets, "head", swap)
    swapped = lax.ppermute(joined, "head", swap)
    total = head_products([targets, partner], joined, swapped, (0,), None)
    below, above, total = ordered((below, above, total))
    far = [lax.ppermute(below[:half], "head", y_shift(1)), lax.ppermute(above[half:], "head", y_shift(-1))]
    pieces = [below, lax.ppermute(below, "head", swap), above, lax.ppermute(above, "head", swap)]
    total = head_products(pieces, joined, swapped, (1, 3), total)
    gram = gram_terms(joined, swapped)
    *far, total, gram = ordered((*far, total, gram))
    far += [lax.ppermute(rows, "head", swap) for rows in far]
    parts = factor_grads(far, joined, swapped, total, gram, targets, up_projection)
    parts = lax.all_to_all(parts, "seq", 0, 0)
    grad_down, grad_up, rel_error = finish(parts, HEAD_COLUMNS, tokens_all)
    return grad_down, grad_up, rel_error.reshape(())


def solution(mesh):
    return jax.shard_map(
        per_device,
        mesh=mesh,
        in_specs=(P("seq", None), P("seq", "head"), P("head", None), P(None, "head"), P("seq")),
        out_specs=(P("seq", "head"), P("seq", "head"), P()),
        check_vma=False,
    )
```
